32 devices in a mesh: sect: 4 (over x, core), tile: 8 (over z, y).
Axes of the slice: x: 2, y: 2, z: 4, core: 2. Of those that a mesh axis runs over, the one named last changes fastest.
Arguments:
- spectrum: float32 [1296, 64, 128], P('sect', 'tile'), may hold values from 0.05 to 1
- courant: float32 [36], replicated, may hold values from 0.1 to 0.45
- group_ratio: float32 [36], replicated, may hold values from 0.5 to 1
- ocean_currents: float32 [2, 16384], P(None, 'tile'), may hold values from -0.15 to 0.15
- elevation: float32 [16384], P('tile'), may hold values from -0.5 to 0.5
- sea_mask: int32 [64, 128], P('tile'), may hold values 0 or 1
- owner_tile: int32 [8192, 1], P('tile'), may hold values from 0 to 7; in each aligned block of 1024 rows (0 to 1023, 1024 to 2047, ...) at most 256 rows name the same one
- ocean_slot: int32 [8192], P('tile'), may hold values from 0 to 2047
Outputs:
- new_spectrum: float32 [1296, 64, 128], P('sect', 'tile')
- ocean_stress: float32 [3, 16384], P(None, 'tile')
The draws below stay inside these ranges and needn't reach their ends.
Inputs may be any that keep to these rules, and one draw needn't show every extreme that they name: `owner_tile`: among the wave cells of one tile at most 256 name the same owner tile, a bound that some block reaches of them.
All inputs are finite; a program needn't handle non-finite values. No bound on the sum of `sea_mask` on one device may be relied on, other than what follows from the above.
Results may differ from the reference program's by a relative error of at most 0.00011.
Values sent between devices are 32-bit elements; how exact they have to be, the bound alone decides.
A program may use at most 64 MiB of HBM per device.

```python
import math
import jax
import jax.numpy as jnp
import numpy as np
from jax import lax

NDIR = 36
NFREQ = 36
STEPS = 4
ROWS = 8
NX = 128
OCT = 2048
BINS = 1296
TILES = 8
NY = 64
CAP = 256
OCEAN = 16384


def place_ends(array, key, least, top_value):
    index_at = [jax.random.randint(jax.random.fold_in(key, axis), (), 0, length) for axis, length in enumerate(array.shape)]
    widest = array.shape.index(max(array.shape))
    beside = index_at[:widest] + [(index_at[widest] + 1) % array.shape[widest]] + index_at[widest + 1:]
    return array.at[tuple(index_at)].set(least).at[tuple(beside)].set(top_value)


def shard_levels(own_key, extent, shards, least, top_value):
    loudness, own = 1.0, jax.random.fold_in(own_key, 6)
    for dim, shards_of in shards:
        heights = jnp.exp(jax.random.uniform(jax.random.fold_in(own, dim), (shards_of,), jnp.float32, least / len(shards), top_value / len(shards)))
        loudness = loudness * jnp.repeat(heights, extent[dim] // shards_of).reshape([-1 if axis == dim else 1 for axis in range(len(extent))])
    return loudness


def assign_block(key, own, number, rows, number_of, top, most, skew):
    order = jax.random.permutation(key, number_of)
    packed, common = shares(number_of, rows * top, most, skew, True), shares(number_of, rows * top, most, skew, False)
    places = jnp.arange(number_of)

    def named(sizes, turn):
        used = int((sizes > 0).sum())
        fixed = max(1, used // 4)
        shifted = fixed + (places - fixed + turn * (used - fixed)) % max(1, number_of - fixed)
        return jnp.zeros((number_of,), jnp.int32).at[order[jnp.where(places < fixed, places, shifted)]].set(jnp.asarray(sizes, jnp.int32))

    sizes = jnp.where(number % 4 == 0, named(packed, number // 4), named(common, number - number // 4 - 1))
    mixed = jax.random.permutation(jax.random.fold_in(own, 3), number_of)
    giver, receiver = mixed[0:number_of // 2 * 2:2], mixed[1:number_of // 2 * 2:2]
    margin = jnp.minimum(sizes[giver] - 1, most - sizes[receiver]) // 2
    margin = jnp.where((giver == order[0]) | (receiver == order[0]) | (sizes[receiver] == 0), 0, jnp.maximum(margin, 0))
    shifted = jax.random.randint(jax.random.fold_in(own, 4), (number_of // 2,), 0, 1 << 20) % (margin + 1)
    sizes = sizes.at[giver].add(-shifted).at[receiver].add(shifted)
    members = jnp.searchsorted(jnp.cumsum(sizes), jnp.arange(rows * top), side="right").astype(jnp.int32)
    table = members.reshape(top, rows).T
    table = table[jax.random.permutation(jax.random.fold_in(own, 1), rows)]
    turn = jax.random.randint(jax.random.fold_in(own, 2), (rows, 1), 0, top)
    return jnp.take_along_axis(table, (jnp.arange(top)[None, :] + turn) % top, axis=1)


def shares(amount, total, reach, lean, full):
    loads = [(1 << 20) // math.isqrt(grade ** lean) + 1 for grade in range(1, amount + 1)]
    largest = reach if full else min(reach, max(-(-total // amount), total * loads[0] // sum(loads)))
    least = 1 if total - largest >= amount - 1 else 0
    holding, surplus = [largest] + [least] * (amount - 1), total - largest - least * (amount - 1)
    while surplus > 0:
        candidates = [i for i in range(1, amount) if holding[i] < largest] or [i for i in range(1, amount) if holding[i] < reach]
        pool, left = sum([loads[i] for i in candidates]), surplus
        for i in candidates:
            addition = min(reach - holding[i], max(1, left * loads[i] // pool), surplus)
            holding[i] = holding[i] + addition
            surplus = surplus - addition
    return np.array(holding)


def setup_inputs(seed: int = 0) -> dict:
    splits = jax.random.split(jax.random.key(seed), 9)
    spectrum = jnp.clip(jnp.exp(math.log(1.0) - 2.9957323 * jax.random.uniform(splits[0], (BINS, NY, NX), jnp.float32) ** shard_levels(splits[0], (BINS, NY, NX), ((0, 4), (1, 8)), -0.2, 0.2)), 0.05, 1.0)
    courant = jnp.clip(jnp.exp(jax.random.uniform(splits[1], (NFREQ,), jnp.float32, math.log(0.1), math.log(0.45))), 0.1, 0.45)
    group_ratio = jnp.clip(jax.random.uniform(splits[2], (NFREQ,), jnp.float32, 0.5, 1.0), 0.5, 1.0)
    ocean_currents = jnp.clip(jax.random.uniform(splits[3], (2, OCEAN), jnp.float32, -0.15, 0.15) * shard_levels(splits[3], (2, OCEAN), ((1, 8),), -0.4, 0.0), -0.15, 0.15)
    elevation = jnp.clip(jax.random.uniform(splits[4], (OCEAN,), jnp.float32, -0.5, 0.5) * shard_levels(splits[4], (OCEAN,), ((0, 8),), -0.4, 0.0), -0.5, 0.5)
    sea_mask = place_ends((jax.random.randint(splits[5], (NY, NX), 0, 4) < 3).astype(jnp.int32), jax.random.fold_in(splits[5], 1), 0, 1)
    owner_tile_keys = jax.random.split(jax.random.fold_in(splits[6], 1), (NY * NX) // (ROWS * NX))
    owner_tile_turns = jax.random.permutation(jax.random.fold_in(splits[6], 3), (NY * NX) // (ROWS * NX))
    owner_tile = jax.vmap(lambda own, number: assign_block(jax.random.fold_in(splits[6], 2), own, number, ROWS * NX, TILES, 1, CAP, 2))(owner_tile_keys, owner_tile_turns).reshape((NY * NX, 1))
    ocean_slot = place_ends(jax.random.randint(splits[7], (NY * NX,), 0, OCT), jax.random.fold_in(splits[7], 1), 0, OCT - 1).astype(jnp.int32)
    return {"spectrum": spectrum, "courant": courant, "group_ratio": group_ratio, "ocean_currents": ocean_currents, "elevation": elevation, "sea_mask": sea_mask, "owner_tile": owner_tile, "ocean_slot": ocean_slot}


def advance(energy, flow_fields, speed_x, speed_y):
    vel_x = speed_x + flow_fields[0]
    vel_y = speed_y + flow_fields[1]
    middle = energy[:, 1:-1]
    mid_vel = vel_x[:, 1:-1]
    face_x = 0.5 * (mid_vel + jnp.roll(mid_vel, -1, axis=2))
    east_side = jnp.roll(middle, -1, axis=2)
    flux_x = jnp.maximum(face_x, 0.0) * middle + jnp.minimum(face_x, 0.0) * east_side
    div_x = flux_x - jnp.roll(flux_x, 1, axis=2)
    face_y = 0.5 * (vel_y[:, :-1] + vel_y[:, 1:])
    flux_y = jnp.maximum(face_y, 0.0) * energy[:, :-1] + jnp.minimum(face_y, 0.0) * energy[:, 1:]
    div_y = flux_y[:, 1:] - flux_y[:, :-1]
    return flow_fields[2, 1:-1] * (middle - div_x - div_y)


def reference(spectrum, courant, group_ratio, ocean_currents, elevation, sea_mask, owner_tile, ocean_slot):
    target = (owner_tile[:, 0] * OCT + ocean_slot).astype(jnp.int32)
    current_at = ocean_currents[:, target]
    eta_at = elevation[target]
    sea_float = sea_mask.astype(jnp.float32)
    flow_fields = jnp.concatenate([current_at.reshape(2, NY, NX), sea_float[None]], 0)
    flow_padded = jnp.pad(flow_fields, ((0, 0), (1, 1), (0, 0)))
    energy = spectrum.reshape(NDIR, NFREQ, NY, NX)

    def one_direction(pieces):
        spectra, dir_id = pieces
        angles = (dir_id.astype(jnp.float32) + 0.5) * (2.0 * math.pi / NDIR)
        cos_dir = jnp.cos(angles)
        sin_dir = jnp.sin(angles)
        speed_x = (courant * cos_dir)[:, None, None]
        speed_y = (courant * sin_dir)[:, None, None]
        for sub_step in range(STEPS):
            spectra = advance(jnp.pad(spectra, ((0, 0), (1, 1), (0, 0))), flow_padded, speed_x, speed_y)
        weights = jnp.stack([group_ratio * (1.0 + cos_dir * cos_dir) - 0.5,
                             group_ratio * cos_dir * sin_dir,
                             group_ratio * (1.0 + sin_dir * sin_dir) - 0.5], 0) * (4.0 / (NDIR * NFREQ))
        partial_value = jnp.dot(weights, spectra.reshape(NFREQ, NY * NX), precision=lax.Precision.HIGHEST)
        return spectra, partial_value

    spectra_all, partials = lax.map(one_direction, (energy, jnp.arange(NDIR, dtype=jnp.int32)))
    stress_w = jnp.sum(partials, 0) * ((1.0 + eta_at) * sea_float.reshape(-1))
    totals = jax.ops.segment_sum(stress_w.T, target, num_segments=OCEAN)
    counts = jax.ops.segment_sum(jnp.ones((NY * NX,), jnp.float32), target, num_segments=OCEAN)
    ocean_stress = (totals / jnp.maximum(counts, 1.0)[:, None]).T
    return spectra_all.reshape(NDIR * NFREQ, NY, NX), ocean_stress
```

```python
import functools
import math

import jax
import jax.numpy as jnp
import numpy as np
from jax import lax
from jax.experimental import pallas as pl
from jax.experimental.pallas import tpu as pltpu
from jax.sharding import PartitionSpec as P

NDIR = 36
NFREQ = 36
STEPS = 4
CHUNKS = 6
UNROLL = 3
MESH = pl.DeviceIdType.MESH
F32 = jnp.float32
BF16 = jnp.bfloat16


def split_bf16(x):
    high = x.astype(BF16)
    return high, (x - high.astype(F32)).astype(BF16)


def lanes_of(x):
    return jnp.concatenate([x[j : j + 1] for j in range(x.shape[0])], axis=1)


def kernel(
    tiles,
    sects,
    cos_ref,
    sin_ref,
    courant_ref,
    ratio_ref,
    current_ref,
    elevation_ref,
    mask_ref,
    owner_ref,
    slot_ref,
    spectrum_ref,
    out_ref,
    stress_ref,
    table,
    energy,
    halo,
    flow,
    scalars,
    parts,
    cells,
    local_sem,
    out_sem,
    halo_send,
    halo_recv,
    table_send,
    table_recv,
    part_send,
    part_recv,
    cell_send,
    cell_recv,
):
    tile = lax.axis_index("tile")
    sect = lax.axis_index("sect")
    bins = spectrum_ref.shape[0]
    rows, columns = mask_ref.shape
    half = rows // 2
    ocean_rows = elevation_ref.shape[0]
    ocean_cells = ocean_rows * columns
    per = bins // CHUNKS
    has_up = tile < tiles - 1
    has_down = tile > 0
    up = lax.rem(tile + 1, tiles)
    down = lax.rem(tile + tiles - 1, tiles)

    load = pltpu.make_async_copy(spectrum_ref, energy, local_sem)
    load.start()

    barrier = pltpu.get_barrier_semaphore()

    @pl.loop(1, tiles)
    def _(k):
        pl.semaphore_signal(
            barrier, inc=1, device_id=(sect, lax.rem(tile + k, tiles)), device_id_type=MESH
        )

    @pl.loop(1, sects)
    def _(k):
        pl.semaphore_signal(
            barrier, inc=1, device_id=(lax.rem(sect + k, sects), tile), device_id_type=MESH
        )

    for r in range(ocean_rows):
        at = pl.ds(r * columns, columns)
        table[tile, pl.ds(r, 1), :] = current_ref[pl.ds(0, 1), at]
        table[tile, pl.ds(ocean_rows + r, 1), :] = current_ref[pl.ds(1, 1), at]
    first = 3 * ocean_rows
    table[tile, pl.ds(2 * ocean_rows, ocean_rows), :] = elevation_ref[...]
    table[tile, pl.ds(first, rows), :] = (owner_ref[...] * ocean_cells + slot_ref[...]).astype(F32)
    table[tile, pl.ds(first + rows, rows), :] = mask_ref[...].astype(F32)

    pl.semaphore_wait(barrier, tiles + sects - 2)

    def table_copy(k, slot):
        return pltpu.make_async_remote_copy(
            src_ref=table.at[tile],
            dst_ref=table.at[slot],
            send_sem=table_send.at[k],
            recv_sem=table_recv.at[slot],
            device_id=(sect, lax.rem(tile + k, tiles)),
            device_id_type=MESH,
        )

    @pl.loop(1, tiles)
    def _(k):
        table_copy(k, tile).start()

    def halo_copy(side, c):
        at = (pl.ds(c * per, per), pl.ds(side * half, half))
        return pltpu.make_async_remote_copy(
            src_ref=spectrum_ref.at[at],
            dst_ref=halo.at[at],
            send_sem=halo_send.at[side, c],
            recv_sem=halo_recv.at[side, c],
            device_id=(sect, down if side == 0 else up),
            device_id_type=MESH,
        )

    for c in range(CHUNKS):

        @pl.when(has_down)
        def _():
            halo_copy(0, c).start()

        @pl.when(has_up)
        def _():
            halo_copy(1, c).start()

    @pl.loop(0, bins)
    def _(b):
        number = sect * bins + b
        d = number // NFREQ
        f = number % NFREQ
        c = cos_ref[d]
        s = sin_ref[d]
        g = courant_ref[f]
        n = ratio_ref[f]
        scale = 4.0 / (NDIR * NFREQ)
        scalars[0, b] = g * c
        scalars[1, b] = g * s
        scalars[2, b] = (n * (1.0 + c * c) - 0.5) * scale
        scalars[3, b] = (n * c * s) * scale
        scalars[4, b] = (n * (1.0 + s * s) - 0.5) * scale

    @pl.loop(1, tiles)
    def _(k):
        table_copy(k, lax.rem(tile + tiles - k, tiles)).wait_recv()

    sub = lax.broadcasted_iota(jnp.int32, (rows, columns), 0)
    upper = sub < half
    valid = (upper & has_up) | (jnp.logical_not(upper) & has_down)

    def ring(start):
        own = table[tile, pl.ds(start, rows), :]
        other = jnp.where(
            upper, table[up, pl.ds(start, rows), :], table[down, pl.ds(start, rows), :]
        )
        return own, other

    target_own, target_halo = ring(first)
    mask_own, mask_halo = ring(first + rows)
    mask_halo = jnp.where(valid, mask_halo, 0.0)
    target_own = target_own.astype(jnp.int32)
    target_halo = target_halo.astype(jnp.int32)

    table_rows = tiles * ocean_rows
    pieces = []
    for field in range(3):
        whole = table[:, pl.ds(field * ocean_rows, ocean_rows), :].reshape(table_rows, columns)
        high, low = split_bf16(whole.T)
        pieces.append(jnp.concatenate([high, low], axis=1))
    lookup = jnp.concatenate(pieces, axis=0)
    row_ids = lax.broadcasted_iota(jnp.int32, (table_rows, 2 * columns), 0)
    lane_ids = lax.broadcasted_iota(jnp.int32, (columns, 2 * columns), 0)
    for j in range(rows):
        index = jnp.concatenate([target_own[j : j + 1], target_halo[j : j + 1]], axis=1)
        hot = jnp.where(row_ids == index // columns, 1.0, 0.0).astype(BF16)
        found = jnp.dot(
            lookup, jnp.concatenate([hot, hot], axis=0), preferred_element_type=F32
        )
        chosen = lane_ids == index % columns
        for field in range(3):
            value = jnp.sum(
                jnp.where(chosen, found[field * columns : (field + 1) * columns], 0.0),
                axis=0,
                keepdims=True,
            )
            flow[field, pl.ds(j, 1), :] = value

    def north(own, other):
        a = pltpu.roll(own, rows - 1, 0)
        b = pltpu.roll(other, rows - 1, 0)
        edge = sub == rows - 1
        return jnp.where(edge, b, a), jnp.where(edge, a, b)

    def south(own, other):
        a = pltpu.roll(own, 1, 0)
        b = pltpu.roll(other, 1, 0)
        edge = sub == 0
        return jnp.where(edge, b, a), jnp.where(edge, a, b)

    def east(x):
        return pltpu.roll(x, columns - 1, 1)

    def west(x):
        return pltpu.roll(x, 1, 1)

    u_own = flow[0, :, pl.ds(0, columns)]
    u_halo = jnp.where(valid, flow[0, :, pl.ds(columns, columns)], 0.0)
    v_own = flow[1, :, pl.ds(0, columns)]
    v_halo = jnp.where(valid, flow[1, :, pl.ds(columns, columns)], 0.0)
    factor = (1.0 + flow[2, :, pl.ds(0, columns)]) * mask_own
    ux_own = 0.5 * (u_own + east(u_own))
    ux_halo = 0.5 * (u_halo + east(u_halo))
    vn_own, vn_halo = north(v_own, v_halo)
    vy_own = 0.5 * (v_own + vn_own)
    vy_halo = 0.5 * (v_halo + vn_halo)

    def one_bin(b):
        e_own = energy[b]
        e_halo = jnp.where(valid, halo[b], 0.0)
        sx = scalars[0, b]
        sy = scalars[1, b]
        ax_own, ax_halo = sx + ux_own, sx + ux_halo
        ay_own, ay_halo = sy + vy_own, sy + vy_halo
        xp_own, xm_own = jnp.maximum(ax_own, 0.0), jnp.minimum(ax_own, 0.0)
        xp_halo, xm_halo = jnp.maximum(ax_halo, 0.0), jnp.minimum(ax_halo, 0.0)
        yp_own, ym_own = jnp.maximum(ay_own, 0.0), jnp.minimum(ay_own, 0.0)
        yp_halo, ym_halo = jnp.maximum(ay_halo, 0.0), jnp.minimum(ay_halo, 0.0)
        for step in range(STEPS):
            n_own, n_halo = north(e_own, e_halo)
            fy_own = yp_own * e_own + ym_own * n_own
            fy_halo = yp_halo * e_halo + ym_halo * n_halo
            s_own, s_halo = south(fy_own, fy_halo)
            fx_own = xp_own * e_own + xm_own * east(e_own)
            if step < STEPS - 1:
                fx_halo = xp_halo * e_halo + xm_halo * east(e_halo)
                e_halo = mask_halo * (e_halo - (fx_halo - west(fx_halo)) - (fy_halo - s_halo))
            e_own = mask_own * (e_own - (fx_own - west(fx_own)) - (fy_own - s_own))
        energy[b] = e_own
        return e_own

    load.wait()
    sums = (jnp.zeros((rows, columns), F32),) * 3
    stores = []
    for c in range(CHUNKS):

        @pl.when(has_up)
        def _():
            halo_copy(0, c).wait_recv()

        @pl.when(has_down)
        def _():
            halo_copy(1, c).wait_recv()

        def body(i, carry):
            for k in range(UNROLL):
                b = c * per + i * UNROLL + k
                e = one_bin(b)
                carry = tuple(carry[q] + scalars[2 + q, b] * e for q in range(3))
            return carry

        sums = lax.fori_loop(0, per // UNROLL, body, sums)
        at = pl.ds(c * per, per)
        store = pltpu.make_async_copy(energy.at[at], out_ref.at[at], out_sem.at[c])
        store.start()
        stores.append(store)

    def part_copy(k, slot):
        return pltpu.make_async_remote_copy(
            src_ref=parts.at[sect],
            dst_ref=parts.at[slot],
            send_sem=part_send.at[k],
            recv_sem=part_recv.at[slot],
            device_id=(lax.rem(sect + k, sects), tile),
            device_id_type=MESH,
        )

    parts[sect] = jnp.concatenate(sums, axis=0)
    for k in range(1, sects):
        part_copy(k, sect).start()
    for k in range(1, sects):
        part_copy(k, lax.rem(sect + sects - k, sects)).wait_recv()
    total = parts[0]
    for k in range(1, sects):
        total = total + parts[k]
    cells[tile] = total * jnp.concatenate([factor] * 3, axis=0)

    def cell_copy(k, slot):
        return pltpu.make_async_remote_copy(
            src_ref=cells.at[tile],
            dst_ref=cells.at[slot],
            send_sem=cell_send.at[k],
            recv_sem=cell_recv.at[slot],
            device_id=(sect, lax.rem(tile + k, tiles)),
            device_id_type=MESH,
        )

    @pl.loop(1, tiles)
    def _(k):
        cell_copy(k, tile).start()

    cell_count = rows * columns
    ocean_ids = lax.broadcasted_iota(jnp.int32, (ocean_rows, cell_count), 0)
    column_ids = lax.broadcasted_iota(jnp.int32, (columns, cell_count), 0)

    def add_tile(source, acc):
        index = lanes_of(table[source, pl.ds(first, rows), :].astype(jnp.int32))
        stress = cells[source]
        row_hot = ocean_ids == index // columns - tile * ocean_rows
        lane_hot = jnp.where(column_ids == index % columns, 1.0, 0.0).astype(BF16)
        highs, lows = [], []
        for k in range(3):
            value = jnp.where(row_hot, lanes_of(stress[k * rows : (k + 1) * rows]), 0.0)
            high, low = split_bf16(value)
            highs.append(high)
            lows.append(low)
        ones = jnp.where(row_hot, 1.0, 0.0).astype(BF16)
        left = jnp.concatenate(highs + lows + [ones], axis=0)
        return acc + lax.dot_general(
            left, lane_hot, (((1,), (1,)), ((), ())), preferred_element_type=F32
        )

    acc = add_tile(tile, jnp.zeros((7 * ocean_rows, columns), F32))

    def add_other(k, acc):
        source = lax.rem(tile + tiles - k, tiles)
        cell_copy(k, source).wait_recv()
        return add_tile(source, acc)

    acc = lax.fori_loop(1, tiles, add_other, acc)
    counts = jnp.maximum(acc[6 * ocean_rows :], 1.0)
    for k in range(3):
        high = acc[k * ocean_rows : (k + 1) * ocean_rows]
        low = acc[(3 + k) * ocean_rows : (4 + k) * ocean_rows]
        mean = (high + low) / counts
        for r in range(ocean_rows):
            stress_ref[pl.ds(k, 1), pl.ds(r * columns, columns)] = mean[r : r + 1]

    for store in stores:
        store.wait()
    for c in range(CHUNKS):

        @pl.when(has_down)
        def _():
            halo_copy(0, c).wait_send()

        @pl.when(has_up)
        def _():
            halo_copy(1, c).wait_send()

    for k in range(1, sects):
        part_copy(k, sect).wait_send()

    @pl.loop(1, tiles)
    def _(k):
        table_copy(k, tile).wait_send()
        cell_copy(k, tile).wait_send()


def local(
    spectrum, courant, group_ratio, ocean_currents, elevation, sea_mask, owner_tile, ocean_slot
):
    bins, rows, columns = spectrum.shape
    tiles = lax.axis_size("tile")
    sects = lax.axis_size("sect")
    ocean_rows = elevation.shape[0] // columns
    angles = (np.arange(NDIR) + 0.5) * (2.0 * math.pi / NDIR)
    smem = pl.BlockSpec(memory_space=pltpu.SMEM)
    vmem = pl.BlockSpec(memory_space=pltpu.VMEM)
    anywhere = pl.BlockSpec(memory_space=pl.ANY)
    dma = pltpu.SemaphoreType.DMA
    return pl.pallas_call(
        functools.partial(kernel, tiles, sects),
        out_shape=(
            jax.ShapeDtypeStruct(spectrum.shape, F32),
            jax.ShapeDtypeStruct((3, elevation.shape[0]), F32),
        ),
        in_specs=[smem] * 4 + [vmem] * 5 + [anywhere],
        out_specs=(anywhere, vmem),
        scratch_shapes=[
            pltpu.VMEM((tiles, 3 * ocean_rows + 2 * rows, columns), F32),
            pltpu.VMEM(spectrum.shape, F32),
            pltpu.VMEM(spectrum.shape, F32),
            pltpu.VMEM((3, rows, 2 * columns), F32),
            pltpu.SMEM((5, bins), F32),
            pltpu.VMEM((sects, 3 * rows, columns), F32),
            pltpu.VMEM((tiles, 3 * rows, columns), F32),
            dma,
            dma((CHUNKS,)),
            dma((2, CHUNKS)),
            dma((2, CHUNKS)),
            dma((tiles,)),
            dma((tiles,)),
            dma((sects,)),
            dma((sects,)),
            dma((tiles,)),
            dma((tiles,)),
        ],
        compiler_params=pltpu.CompilerParams(
            collective_id=0, has_side_effects=True, vmem_limit_bytes=48 * 1024 * 1024
        ),
        cost_estimate=pl.CostEstimate(
            flops=bins * rows * columns * 200, bytes_accessed=8 * bins * rows * columns,
            transcendentals=0,
        ),
        name="coupling",
    )(
        jnp.asarray(np.cos(angles), F32),
        jnp.asarray(np.sin(angles), F32),
        courant,
        group_ratio,
        ocean_currents,
        elevation.reshape(ocean_rows, columns),
        sea_mask,
        owner_tile.reshape(rows, columns),
        ocean_slot.reshape(rows, columns),
        spectrum,
    )


def solution(mesh):
    in_specs = (
        P("sect", "tile", None),
        P(),
        P(),
        P(None, "tile"),
        P("tile"),
        P("tile", None),
        P("tile", None),
        P("tile"),
    )
    out_specs = (P("sect", "tile", None), P(None, "tile"))
    return jax.shard_map(local, mesh=mesh, in_specs=in_specs, out_specs=out_specs, check_vma=False)
```

```python
import functools
import math

import jax
import jax.numpy as jnp
import numpy as np
from jax import lax
from jax.experimental import pallas as pl
from jax.experimental.pallas import tpu as pltpu
from jax.sharding import PartitionSpec as P

NDIR = 36
NFREQ = 36
STEPS = 4
CHUNKS = 8
GROUP = 8
MESH = pl.DeviceIdType.MESH
F32 = jnp.float32
BF16 = jnp.bfloat16


def split_bf16(x):
    high = x.astype(BF16)
    return high, (x - high.astype(F32)).astype(BF16)


def lanes_of(x):
    return jnp.concatenate([x[j : j + 1] for j in range(x.shape[0])], axis=1)


def chunk_bounds(groups):
    return [groups * c // CHUNKS for c in range(CHUNKS + 1)]


def kernel(
    tiles,
    sects,
    trig_hbm,
    courant_hbm,
    ratio_hbm,
    current_hbm,
    elevation_hbm,
    mask_hbm,
    owner_hbm,
    slot_hbm,
    spectrum_ref,
    out_ref,
    stress_ref,
    trig_ref,
    courant_ref,
    ratio_ref,
    current_ref,
    mask_ref,
    owner_ref,
    slot_ref,
    table,
    energy,
    result,
    halo,
    flow,
    fields,
    scalars,
    sums,
    parts,
    cells,
    small_sem,
    load_sem,
    out_sem,
    halo_send,
    halo_recv,
    table_send,
    table_recv,
    part_send,
    part_recv,
    cell_send,
    cell_recv,
):
    tile = lax.axis_index("tile")
    sect = lax.axis_index("sect")
    bins = spectrum_ref.shape[0]
    rows, columns = mask_ref.shape
    half = rows // 2
    ocean_rows = elevation_hbm.shape[0]
    ocean_cells = ocean_rows * columns
    groups = halo.shape[0] // GROUP
    bounds = chunk_bounds(groups)
    first = 3 * ocean_rows
    shift = columns.bit_length() - 1
    has_up = tile < tiles - 1
    has_down = tile > 0
    up = lax.rem(tile + 1, tiles)
    down = lax.rem(tile + tiles - 1, tiles)

    small = [
        (trig_hbm, trig_ref),
        (courant_hbm, courant_ref),
        (ratio_hbm, ratio_ref),
        (current_hbm, current_ref),
        (elevation_hbm, table.at[tile, pl.ds(2 * ocean_rows, ocean_rows)]),
        (mask_hbm, mask_ref),
        (owner_hbm, owner_ref),
        (slot_hbm, slot_ref),
    ]
    small = [pltpu.make_async_copy(a, b, small_sem.at[i]) for i, (a, b) in enumerate(small)]
    for copy in small:
        copy.start()
    load = pltpu.make_async_copy(spectrum_ref, energy.at[pl.ds(0, bins)], load_sem)
    load.start()

    barrier = pltpu.get_barrier_semaphore()

    @pl.loop(1, tiles)
    def _(k):
        pl.semaphore_signal(
            barrier, inc=1, device_id=(sect, lax.rem(tile + k, tiles)), device_id_type=MESH
        )

    @pl.loop(1, sects)
    def _(k):
        pl.semaphore_signal(
            barrier, inc=1, device_id=(lax.rem(sect + k, sects), tile), device_id_type=MESH
        )

    for copy in small:
        copy.wait()
    for r in range(ocean_rows):
        at = pl.ds(r * columns, columns)
        table[tile, pl.ds(r, 1), :] = current_ref[pl.ds(0, 1), at]
        table[tile, pl.ds(ocean_rows + r, 1), :] = current_ref[pl.ds(1, 1), at]
    table[tile, pl.ds(first, rows), :] = (owner_ref[...] * ocean_cells + slot_ref[...]).astype(F32)
    table[tile, pl.ds(first + rows, rows), :] = mask_ref[...].astype(F32)

    pl.semaphore_wait(barrier, tiles + sects - 2)

    def table_copy(k, slot):
        return pltpu.make_async_remote_copy(
            src_ref=table.at[tile],
            dst_ref=table.at[slot],
            send_sem=table_send.at[k],
            recv_sem=table_recv.at[slot],
            device_id=(sect, lax.rem(tile + k, tiles)),
            device_id_type=MESH,
        )

    @pl.loop(1, tiles)
    def _(k):
        table_copy(k, tile).start()

    def halo_copy(side, c):
        begin, end = bounds[c] * GROUP, min(bounds[c + 1] * GROUP, bins)
        at = (pl.ds(begin, end - begin), pl.ds(side * half, half))
        return pltpu.make_async_remote_copy(
            src_ref=spectrum_ref.at[at],
            dst_ref=halo.at[at],
            send_sem=halo_send.at[side, c],
            recv_sem=halo_recv.at[side, c],
            device_id=(sect, down if side == 0 else up),
            device_id_type=MESH,
        )

    for c in range(CHUNKS):

        @pl.when(has_down)
        def _():
            halo_copy(0, c).start()

        @pl.when(has_up)
        def _():
            halo_copy(1, c).start()

    def fill(b, place):
        d, f = place
        c = trig_ref[d]
        s = trig_ref[NDIR + d]
        g = courant_ref[f]
        n = ratio_ref[f]
        scale = 4.0 / (NDIR * NFREQ)
        values = (
            g * c,
            g * s,
            (n * (1.0 + c * c) - 0.5) * scale,
            (n * c * s) * scale,
            (n * (1.0 + s * s) - 0.5) * scale,
        )
        for q in range(5):
            scalars[q, pl.ds(b, 1), :] = jnp.full((1, columns), values[q], F32)
        last = f == NFREQ - 1
        return jnp.where(last, d + 1, d), jnp.where(last, 0, f + 1)

    start = sect * bins
    lax.fori_loop(0, bins, fill, (start // NFREQ, start % NFREQ))
    spare = groups * GROUP - bins
    if spare:
        for q in range(5):
            scalars[q, pl.ds(bins, spare), :] = jnp.zeros((spare, columns), F32)
        for b in range(bins, bins + spare):
            energy[b] = jnp.zeros((rows, columns), F32)
            halo[b] = jnp.zeros((rows, columns), F32)
    sums[...] = jnp.zeros_like(sums)

    @pl.loop(1, tiles)
    def _(k):
        table_copy(k, lax.rem(tile + tiles - k, tiles)).wait_recv()

    sub = lax.broadcasted_iota(jnp.int32, (rows, columns), 0)
    upper = sub < half
    valid = (upper & has_up) | (jnp.logical_not(upper) & has_down)

    def ring(start):
        own = table[tile, pl.ds(start, rows), :]
        other = jnp.where(
            upper, table[up, pl.ds(start, rows), :], table[down, pl.ds(start, rows), :]
        )
        return own, other

    target_own, target_halo = ring(first)
    mask_own, mask_halo = ring(first + rows)
    mask_halo = jnp.where(valid, mask_halo, 0.0)
    target_own = target_own.astype(jnp.int32)
    target_halo = target_halo.astype(jnp.int32)

    table_rows = tiles * ocean_rows
    pieces = []
    for field in range(3):
        whole = table[:, pl.ds(field * ocean_rows, ocean_rows), :].reshape(table_rows, columns)
        high, low = split_bf16(whole.T)
        pieces.append(jnp.concatenate([high, low], axis=1))
    lookup = jnp.concatenate(pieces, axis=0)
    row_ids = lax.broadcasted_iota(jnp.int32, (table_rows, 2 * columns), 0)
    lane_ids = lax.broadcasted_iota(jnp.int32, (columns, 2 * columns), 0)
    for j in range(rows):
        index = jnp.concatenate([target_own[j : j + 1], target_halo[j : j + 1]], axis=1)
        hot = jnp.where(row_ids == index >> shift, 1.0, 0.0).astype(BF16)
        found = jnp.dot(
            lookup, jnp.concatenate([hot, hot], axis=0), preferred_element_type=F32
        )
        chosen = lane_ids == (index & (columns - 1))
        for field in range(3):
            value = jnp.sum(
                jnp.where(chosen, found[field * columns : (field + 1) * columns], 0.0),
                axis=0,
                keepdims=True,
            )
            flow[field, pl.ds(j, 1), :] = value

    def east(x):
        return pltpu.roll(x, columns - 1, 1)

    def west(x):
        return pltpu.roll(x, 1, 1)

    u_own = flow[0, :, pl.ds(0, columns)]
    u_halo = jnp.where(valid, flow[0, :, pl.ds(columns, columns)], 0.0)
    v_own = flow[1, :, pl.ds(0, columns)]
    v_halo = jnp.where(valid, flow[1, :, pl.ds(columns, columns)], 0.0)
    factor = (1.0 + flow[2, :, pl.ds(0, columns)]) * mask_own
    extent = rows + 2 * half

    def in_order(own, other):
        return jnp.concatenate([other[half:], own, other[:half]], axis=0)

    u_all = in_order(u_own, u_halo)
    v_all = in_order(v_own, v_halo)
    m_all = in_order(mask_own, mask_halo)
    ux_all = 0.5 * (u_all + east(u_all))
    uw_all = west(ux_all)
    vy_all = 0.5 * (v_all[:-1] + v_all[1:])
    for j in range(extent):
        fields[0, j] = jnp.broadcast_to(ux_all[j : j + 1], (GROUP, columns))
        fields[1, j] = jnp.broadcast_to(uw_all[j : j + 1], (GROUP, columns))
        fields[2, j] = jnp.broadcast_to(m_all[j : j + 1], (GROUP, columns))
        if j < extent - 1:
            fields[3, j] = jnp.broadcast_to(vy_all[j : j + 1], (GROUP, columns))

    lines = bins + spare
    energy_rows = energy.reshape(lines * rows, columns)
    halo_rows = halo.reshape(lines * rows, columns)
    result_rows = result.reshape(lines * rows, columns)

    def one_group(g, _):
        begin = g * GROUP
        base = begin * rows
        e = {}
        for j in range(rows):
            place = base + j
            e[half + j] = energy_rows[pl.ds(place, GROUP, stride=rows), :]
            outside = halo_rows[pl.ds(place, GROUP, stride=rows), :]
            if j < half:
                e[half + rows + j] = jnp.where(has_up, outside, 0.0)
            else:
                e[j - half] = jnp.where(has_down, outside, 0.0)
        sx = scalars[0, pl.ds(begin, GROUP), :]
        sy = scalars[1, pl.ds(begin, GROUP), :]
        yp, ym, xm, xpw, c0 = {}, {}, {}, {}, {}
        for j in range(extent - 1):
            ay = sy + fields[3, j]
            yp[j], ym[j] = jnp.maximum(ay, 0.0), jnp.minimum(ay, 0.0)
        for j in range(1, extent - 1):
            ax = sx + fields[0, j]
            aw = sx + fields[1, j]
            xm[j] = jnp.minimum(ax, 0.0)
            xpw[j] = jnp.maximum(aw, 0.0)
            c0[j] = (1.0 - jnp.maximum(ax, 0.0) + jnp.minimum(aw, 0.0)) - (yp[j] - ym[j - 1])
        for step in range(1, STEPS + 1):
            new = {}
            for j in range(step, extent - step):
                value = c0[j] * e[j] - xm[j] * east(e[j]) + xpw[j] * west(e[j])
                value = value - ym[j] * e[j + 1] + yp[j - 1] * e[j - 1]
                new[j] = fields[2, j] * value
            e = new
        weights = [scalars[2 + k, pl.ds(begin, GROUP), :] for k in range(3)]
        for j in range(rows):
            final = e[half + j]
            result_rows[pl.ds(base + j, GROUP, stride=rows), :] = final
            for k in range(3):
                sums[k, j] += weights[k] * final
        return 0

    load.wait()
    stores = []
    for c in range(CHUNKS):

        @pl.when(has_up)
        def _():
            halo_copy(0, c).wait_recv()

        @pl.when(has_down)
        def _():
            halo_copy(1, c).wait_recv()

        lax.fori_loop(bounds[c], bounds[c + 1], one_group, 0)
        begin, end = bounds[c] * GROUP, min(bounds[c + 1] * GROUP, bins)
        at = pl.ds(begin, end - begin)
        store = pltpu.make_async_copy(result.at[at], out_ref.at[at], out_sem.at[c])
        store.start()
        stores.append(store)

    def part_copy(k, slot):
        return pltpu.make_async_remote_copy(
            src_ref=parts.at[sect],
            dst_ref=parts.at[slot],
            send_sem=part_send.at[k],
            recv_sem=part_recv.at[slot],
            device_id=(lax.rem(sect + k, sects), tile),
            device_id_type=MESH,
        )

    for k in range(3):
        for j in range(rows):
            parts[sect, pl.ds(k * rows + j, 1), :] = jnp.sum(sums[k, j], axis=0, keepdims=True)
    for k in range(1, sects):
        part_copy(k, sect).start()
    for k in range(1, sects):
        part_copy(k, lax.rem(sect + sects - k, sects)).wait_recv()
    total = parts[0]
    for k in range(1, sects):
        total = total + parts[k]
    cells[tile] = total * jnp.concatenate([factor] * 3, axis=0)

    def cell_copy(k, slot):
        return pltpu.make_async_remote_copy(
            src_ref=cells.at[tile],
            dst_ref=cells.at[slot],
            send_sem=cell_send.at[k],
            recv_sem=cell_recv.at[slot],
            device_id=(sect, lax.rem(tile + k, tiles)),
            device_id_type=MESH,
        )

    @pl.loop(1, tiles)
    def _(k):
        cell_copy(k, tile).start()

    cell_count = rows * columns
    ocean_ids = lax.broadcasted_iota(jnp.int32, (ocean_rows, cell_count), 0)
    column_ids = lax.broadcasted_iota(jnp.int32, (columns, cell_count), 0)

    def add_tile(source, acc):
        index = lanes_of(table[source, pl.ds(first, rows), :].astype(jnp.int32))
        stress = cells[source]
        row_hot = ocean_ids == (index >> shift) - tile * ocean_rows
        lane_hot = jnp.where(column_ids == (index & (columns - 1)), 1.0, 0.0).astype(BF16)
        highs, lows = [], []
        for k in range(3):
            value = jnp.where(row_hot, lanes_of(stress[k * rows : (k + 1) * rows]), 0.0)
            high, low = split_bf16(value)
            highs.append(high)
            lows.append(low)
        ones = jnp.where(row_hot, 1.0, 0.0).astype(BF16)
        left = jnp.concatenate(highs + lows + [ones], axis=0)
        return acc + lax.dot_general(
            left, lane_hot, (((1,), (1,)), ((), ())), preferred_element_type=F32
        )

    acc = add_tile(tile, jnp.zeros((7 * ocean_rows, columns), F32))

    def add_other(k, acc):
        source = lax.rem(tile + tiles - k, tiles)
        cell_copy(k, source).wait_recv()
        return add_tile(source, acc)

    acc = lax.fori_loop(1, tiles, add_other, acc)
    counts = jnp.maximum(acc[6 * ocean_rows :], 1.0)
    for k in range(3):
        high = acc[k * ocean_rows : (k + 1) * ocean_rows]
        low = acc[(3 + k) * ocean_rows : (4 + k) * ocean_rows]
        mean = (high + low) / counts
        for r in range(ocean_rows):
            stress_ref[pl.ds(k, 1), pl.ds(r * columns, columns)] = mean[r : r + 1]

    for store in stores:
        store.wait()
    for c in range(CHUNKS):

        @pl.when(has_down)
        def _():
            halo_copy(0, c).wait_send()

        @pl.when(has_up)
        def _():
            halo_copy(1, c).wait_send()

    for k in range(1, sects):
        part_copy(k, sect).wait_send()

    @pl.loop(1, tiles)
    def _(k):
        table_copy(k, tile).wait_send()
        cell_copy(k, tile).wait_send()


def local(
    spectrum, courant, group_ratio, ocean_currents, elevation, sea_mask, owner_tile, ocean_slot
):
    bins, rows, columns = spectrum.shape
    tiles = lax.axis_size("tile")
    sects = lax.axis_size("sect")
    ocean_rows = elevation.shape[0] // columns
    angles = (np.arange(NDIR) + 0.5) * (2.0 * math.pi / NDIR)
    lines = -(-bins // GROUP) * GROUP
    extent = 2 * rows
    vmem = pl.BlockSpec(memory_space=pltpu.VMEM)
    hbm = pl.BlockSpec(memory_space=pltpu.HBM)
    dma = pltpu.SemaphoreType.DMA
    return pl.pallas_call(
        functools.partial(kernel, tiles, sects),
        out_shape=(
            jax.ShapeDtypeStruct(spectrum.shape, F32),
            jax.ShapeDtypeStruct((3, elevation.shape[0]), F32),
        ),
        in_specs=[hbm] * 9,
        out_specs=(hbm, vmem),
        scratch_shapes=[
            pltpu.SMEM((2 * NDIR,), F32),
            pltpu.SMEM((NFREQ,), F32),
            pltpu.SMEM((NFREQ,), F32),
            pltpu.VMEM(ocean_currents.shape, F32),
            pltpu.VMEM((rows, columns), jnp.int32),
            pltpu.VMEM((rows, columns), jnp.int32),
            pltpu.VMEM((rows, columns), jnp.int32),
            pltpu.VMEM((tiles, 3 * ocean_rows + 2 * rows, columns), F32),
            pltpu.VMEM((lines, rows, columns), F32),
            pltpu.VMEM((lines, rows, columns), F32),
            pltpu.VMEM((lines, rows, columns), F32),
            pltpu.VMEM((3, rows, 2 * columns), F32),
            pltpu.VMEM((4, extent, GROUP, columns), F32),
            pltpu.VMEM((5, lines, columns), F32),
            pltpu.VMEM((3, rows, GROUP, columns), F32),
            pltpu.VMEM((sects, 3 * rows, columns), F32),
            pltpu.VMEM((tiles, 3 * rows, columns), F32),
            dma((8,)),
            dma,
            dma((CHUNKS,)),
            dma((2, CHUNKS)),
            dma((2, CHUNKS)),
            dma((tiles,)),
            dma((tiles,)),
            dma((sects,)),
            dma((sects,)),
            dma((tiles,)),
            dma((tiles,)),
        ],
        compiler_params=pltpu.CompilerParams(
            collective_id=0, has_side_effects=True, vmem_limit_bytes=60 * 1024 * 1024
        ),
        cost_estimate=pl.CostEstimate(
            flops=bins * rows * columns * 200, bytes_accessed=8 * bins * rows * columns,
            transcendentals=0,
        ),
        name="coupling",
    )(
        jnp.asarray(np.concatenate([np.cos(angles), np.sin(angles)]), F32),
        courant,
        group_ratio,
        ocean_currents,
        elevation.reshape(ocean_rows, columns),
        sea_mask,
        owner_tile.reshape(rows, columns),
        ocean_slot.reshape(rows, columns),
        spectrum,
    )


def solution(mesh):
    in_specs = (
        P("sect", "tile", None),
        P(),
        P(),
        P(None, "tile"),
        P("tile"),
        P("tile", None),
        P("tile", None),
        P("tile"),
    )
    out_specs = (P("sect", "tile", None), P(None, "tile"))
    return jax.shard_map(local, mesh=mesh, in_specs=in_specs, out_specs=out_specs, check_vma=False)
```

```python
import functools
import math

import jax
import jax.numpy as jnp
import numpy as np
from jax import lax
from jax.experimental import pallas as pl
from jax.experimental.pallas import tpu as pltpu
from jax.sharding import PartitionSpec as P

NDIR = 36
NFREQ = 36
STEPS = 4
CHUNKS = 8
SHARES = (0, 6, 12, 18, 24, 30, 35, 39, 41)
GROUP = 8
MESH = pl.DeviceIdType.MESH
F32 = jnp.float32
BF16 = jnp.bfloat16


def split_bf16(x):
    high = x.astype(BF16)
    return high, (x - high.astype(F32)).astype(BF16)


def lanes_of(x):
    return jnp.concatenate([x[j : j + 1] for j in range(x.shape[0])], axis=1)


def chunk_bounds(groups):
    return [groups * share // SHARES[-1] for share in SHARES]


def kernel(
    tiles,
    sects,
    trig_hbm,
    courant_hbm,
    ratio_hbm,
    current_hbm,
    elevation_hbm,
    mask_hbm,
    owner_hbm,
    slot_hbm,
    spectrum_ref,
    out_ref,
    stress_ref,
    trig_ref,
    courant_ref,
    ratio_ref,
    current_ref,
    mask_ref,
    owner_ref,
    slot_ref,
    table,
    energy,
    result,
    halo,
    flow,
    fields,
    scalars,
    by_freq,
    hots,
    sums,
    parts,
    cells,
    small_sem,
    load_sem,
    out_sem,
    halo_send,
    halo_recv,
    table_send,
    table_recv,
    part_send,
    part_recv,
    cell_send,
    cell_recv,
):
    tile = lax.axis_index("tile")
    sect = lax.axis_index("sect")
    bins = spectrum_ref.shape[0]
    rows, columns = mask_ref.shape
    half = rows // 2
    ocean_rows = elevation_hbm.shape[0]
    ocean_cells = ocean_rows * columns
    groups = halo.shape[0] // GROUP
    bounds = chunk_bounds(groups)
    first = 3 * ocean_rows
    shift = columns.bit_length() - 1
    has_up = tile < tiles - 1
    has_down = tile > 0
    up = lax.rem(tile + 1, tiles)
    down = lax.rem(tile + tiles - 1, tiles)

    small = [
        (trig_hbm, trig_ref),
        (courant_hbm, courant_ref),
        (ratio_hbm, ratio_ref),
        (current_hbm, current_ref),
        (elevation_hbm, table.at[tile, pl.ds(2 * ocean_rows, ocean_rows)]),
        (mask_hbm, mask_ref),
        (owner_hbm, owner_ref),
        (slot_hbm, slot_ref),
    ]
    small = [pltpu.make_async_copy(a, b, small_sem.at[i]) for i, (a, b) in enumerate(small)]
    for copy in small:
        copy.start()
    load = pltpu.make_async_copy(spectrum_ref, energy.at[pl.ds(0, bins)], load_sem)
    load.start()

    barrier = pltpu.get_barrier_semaphore()

    @pl.loop(1, tiles)
    def _(k):
        pl.semaphore_signal(
            barrier, inc=1, device_id=(sect, lax.rem(tile + k, tiles)), device_id_type=MESH
        )

    @pl.loop(1, sects)
    def _(k):
        pl.semaphore_signal(
            barrier, inc=1, device_id=(lax.rem(sect + k, sects), tile), device_id_type=MESH
        )

    for copy in small:
        copy.wait()
    for r in range(ocean_rows):
        at = pl.ds(r * columns, columns)
        table[tile, pl.ds(r, 1), :] = current_ref[pl.ds(0, 1), at]
        table[tile, pl.ds(ocean_rows + r, 1), :] = current_ref[pl.ds(1, 1), at]
    table[tile, pl.ds(first, rows), :] = (owner_ref[...] * ocean_cells + slot_ref[...]).astype(F32)
    table[tile, pl.ds(first + rows, rows), :] = mask_ref[...].astype(F32)

    pl.semaphore_wait(barrier, tiles + sects - 2)

    def table_copy(k, slot):
        return pltpu.make_async_remote_copy(
            src_ref=table.at[tile],
            dst_ref=table.at[slot],
            send_sem=table_send.at[k],
            recv_sem=table_recv.at[slot],
            device_id=(sect, lax.rem(tile + k, tiles)),
            device_id_type=MESH,
        )

    @pl.loop(1, tiles)
    def _(k):
        table_copy(k, tile).start()

    def halo_copy(side, c):
        begin, end = bounds[c] * GROUP, min(bounds[c + 1] * GROUP, bins)
        at = (pl.ds(begin, end - begin), pl.ds(side * half, half))
        return pltpu.make_async_remote_copy(
            src_ref=spectrum_ref.at[at],
            dst_ref=halo.at[at],
            send_sem=halo_send.at[side, c],
            recv_sem=halo_recv.at[side, c],
            device_id=(sect, down if side == 0 else up),
            device_id_type=MESH,
        )

    for c in range(CHUNKS):

        @pl.when(has_down)
        def _():
            halo_copy(0, c).start()

        @pl.when(has_up)
        def _():
            halo_copy(1, c).start()

    start = sect * bins
    first_dir, first_freq = start // NFREQ, start % NFREQ
    for i in range(NFREQ):
        f = first_freq + i
        f = jnp.where(f >= NFREQ, f - NFREQ, f)
        by_freq[0, pl.ds(i, 1), :] = jnp.full((1, columns), courant_ref[f], F32)
        by_freq[1, pl.ds(i, 1), :] = jnp.full((1, columns), ratio_ref[f], F32)
    speed, ratio = by_freq[0], by_freq[1]
    wrapped = lax.broadcasted_iota(jnp.int32, (NFREQ, columns), 0) + first_freq >= NFREQ
    scale = 4.0 / (NDIR * NFREQ)
    for begin in range(0, bins, NFREQ):
        count = min(NFREQ, bins - begin)
        d = first_dir + begin // NFREQ
        c = jnp.where(wrapped, trig_ref[d + 1], trig_ref[d])
        s = jnp.where(wrapped, trig_ref[NDIR + d + 1], trig_ref[NDIR + d])
        values = (
            speed * c,
            speed * s,
            (ratio * (1.0 + c * c) - 0.5) * scale,
            (ratio * c * s) * scale,
            (ratio * (1.0 + s * s) - 0.5) * scale,
        )
        for q in range(5):
            scalars[q, pl.ds(begin, count), :] = values[q][:count]
    spare = groups * GROUP - bins
    if spare:
        for q in range(5):
            scalars[q, pl.ds(bins, spare), :] = jnp.zeros((spare, columns), F32)
        for b in range(bins, bins + spare):
            energy[b] = jnp.zeros((rows, columns), F32)
            halo[b] = jnp.zeros((rows, columns), F32)
    sums[...] = jnp.zeros_like(sums)

    @pl.loop(1, tiles)
    def _(k):
        table_copy(k, lax.rem(tile + tiles - k, tiles)).wait_recv()

    sub = lax.broadcasted_iota(jnp.int32, (rows, columns), 0)
    upper = sub < half
    valid = (upper & has_up) | (jnp.logical_not(upper) & has_down)

    def ring(start):
        own = table[tile, pl.ds(start, rows), :]
        other = jnp.where(
            upper, table[up, pl.ds(start, rows), :], table[down, pl.ds(start, rows), :]
        )
        return own, other

    target_own, target_halo = ring(first)
    mask_own, mask_halo = ring(first + rows)
    mask_halo = jnp.where(valid, mask_halo, 0.0)
    target_own = target_own.astype(jnp.int32)
    target_halo = target_halo.astype(jnp.int32)

    table_rows = tiles * ocean_rows
    pieces = []
    for field in range(3):
        whole = table[:, pl.ds(field * ocean_rows, ocean_rows), :].reshape(table_rows, columns)
        high, low = split_bf16(whole.T)
        pieces.append(jnp.concatenate([high, low], axis=1))
    lookup = jnp.concatenate(pieces, axis=0)
    row_ids = lax.broadcasted_iota(jnp.int32, (table_rows, 2 * columns), 0)
    lane_ids = lax.broadcasted_iota(jnp.int32, (columns, 2 * columns), 0)
    for j in range(rows):
        index = jnp.concatenate([target_own[j : j + 1], target_halo[j : j + 1]], axis=1)
        hot = jnp.where(row_ids == index >> shift, 1.0, 0.0).astype(BF16)
        found = jnp.dot(
            lookup, jnp.concatenate([hot, hot], axis=0), preferred_element_type=F32
        )
        chosen = lane_ids == (index & (columns - 1))
        for field in range(3):
            value = jnp.sum(
                jnp.where(chosen, found[field * columns : (field + 1) * columns], 0.0),
                axis=0,
                keepdims=True,
            )
            flow[field, pl.ds(j, 1), :] = value

    def east(x):
        return pltpu.roll(x, columns - 1, 1)

    def west(x):
        return pltpu.roll(x, 1, 1)

    u_own = flow[0, :, pl.ds(0, columns)]
    u_halo = jnp.where(valid, flow[0, :, pl.ds(columns, columns)], 0.0)
    v_own = flow[1, :, pl.ds(0, columns)]
    v_halo = jnp.where(valid, flow[1, :, pl.ds(columns, columns)], 0.0)
    factor = (1.0 + flow[2, :, pl.ds(0, columns)]) * mask_own
    extent = rows + 2 * half

    def in_order(own, other):
        return jnp.concatenate([other[half:], own, other[:half]], axis=0)

    u_all = in_order(u_own, u_halo)
    v_all = in_order(v_own, v_halo)
    m_all = in_order(mask_own, mask_halo)
    ux_all = 0.5 * (u_all + east(u_all))
    uw_all = west(ux_all)
    vy_all = 0.5 * (v_all[:-1] + v_all[1:])
    for j in range(extent):
        fields[0, j] = jnp.broadcast_to(ux_all[j : j + 1], (GROUP, columns))
        fields[1, j] = jnp.broadcast_to(uw_all[j : j + 1], (GROUP, columns))
        fields[2, j] = jnp.broadcast_to(m_all[j : j + 1], (GROUP, columns))
        if j < extent - 1:
            fields[3, j] = jnp.broadcast_to(vy_all[j : j + 1], (GROUP, columns))

    lines = bins + spare
    energy_rows = energy.reshape(lines * rows, columns)
    halo_rows = halo.reshape(lines * rows, columns)
    result_rows = result.reshape(lines * rows, columns)

    def one_group(g, _):
        begin = g * GROUP
        base = begin * rows
        e = {}
        for j in range(rows):
            place = base + j
            e[half + j] = energy_rows[pl.ds(place, GROUP, stride=rows), :]
            outside = halo_rows[pl.ds(place, GROUP, stride=rows), :]
            if j < half:
                e[half + rows + j] = jnp.where(has_up, outside, 0.0)
            else:
                e[j - half] = jnp.where(has_down, outside, 0.0)
        sx = scalars[0, pl.ds(begin, GROUP), :]
        sy = scalars[1, pl.ds(begin, GROUP), :]
        yp, ym, xm, xpw, c0 = {}, {}, {}, {}, {}

        def coefficients(j):
            ay = sy + fields[3, j]
            yp[j], ym[j] = jnp.maximum(ay, 0.0), jnp.minimum(ay, 0.0)
            if j:
                ax = sx + fields[0, j]
                aw = sx + fields[1, j]
                xm[j] = jnp.minimum(ax, 0.0)
                xpw[j] = jnp.maximum(aw, 0.0)
                c0[j] = (1.0 - jnp.maximum(ax, 0.0) + jnp.minimum(aw, 0.0)) - (yp[j] - ym[j - 1])

        levels = [e] + [{} for _ in range(STEPS)]
        coefficients(0)
        for wave in range(1, extent + 2 * STEPS):
            if wave < extent - 1:
                coefficients(wave)
            for step in range(STEPS, 0, -1):
                j = wave - 2 * (step - 1)
                if step <= j < extent - step:
                    old = levels[step - 1]
                    value = c0[j] * old[j] - xm[j] * east(old[j]) + xpw[j] * west(old[j])
                    value = value - ym[j] * old[j + 1] + yp[j - 1] * old[j - 1]
                    levels[step][j] = fields[2, j] * value
        e = levels[STEPS]
        weights = [scalars[2 + k, pl.ds(begin, GROUP), :] for k in range(3)]
        for j in range(rows):
            final = e[half + j]
            result_rows[pl.ds(base + j, GROUP, stride=rows), :] = final
            for k in range(3):
                sums[k, j] += weights[k] * final
        return 0

    load.wait()
    stores = []
    for c in range(CHUNKS):

        @pl.when(has_up)
        def _():
            halo_copy(0, c).wait_recv()

        @pl.when(has_down)
        def _():
            halo_copy(1, c).wait_recv()

        lax.fori_loop(bounds[c], bounds[c + 1], one_group, 0)
        begin, end = bounds[c] * GROUP, min(bounds[c + 1] * GROUP, bins)
        at = pl.ds(begin, end - begin)
        store = pltpu.make_async_copy(result.at[at], out_ref.at[at], out_sem.at[c])
        store.start()
        stores.append(store)

    def part_copy(k, slot):
        return pltpu.make_async_remote_copy(
            src_ref=parts.at[sect],
            dst_ref=parts.at[slot],
            send_sem=part_send.at[k],
            recv_sem=part_recv.at[slot],
            device_id=(lax.rem(sect + k, sects), tile),
            device_id_type=MESH,
        )

    for k in range(3):
        for j in range(rows):
            parts[sect, pl.ds(k * rows + j, 1), :] = jnp.sum(sums[k, j], axis=0, keepdims=True)
    for k in range(1, sects):
        part_copy(k, sect).start()

    cell_count = rows * columns
    ocean_ids = lax.broadcasted_iota(jnp.int32, (ocean_rows, cell_count), 0) + tile * ocean_rows

    def index_of(source):
        return lanes_of(table[source, pl.ds(first, rows), :].astype(jnp.int32))

    def row_hot_of(source):
        return ocean_ids == index_of(source) >> shift

    @pl.loop(0, tiles)
    def _(source):
        lane = index_of(source) & (columns - 1)
        ids = lax.broadcasted_iota(jnp.int32, (columns, cell_count), 0)
        hots[source] = jnp.where(ids == lane, 1.0, 0.0).astype(BF16)

    for k in range(1, sects):
        part_copy(k, lax.rem(sect + sects - k, sects)).wait_recv()
    total = parts[0]
    for k in range(1, sects):
        total = total + parts[k]
    cells[tile] = total * jnp.concatenate([factor] * 3, axis=0)

    def cell_copy(k, slot):
        return pltpu.make_async_remote_copy(
            src_ref=cells.at[tile],
            dst_ref=cells.at[slot],
            send_sem=cell_send.at[k],
            recv_sem=cell_recv.at[slot],
            device_id=(sect, lax.rem(tile + k, tiles)),
            device_id_type=MESH,
        )

    @pl.loop(1, tiles)
    def _(k):
        cell_copy(k, tile).start()

    def product(left, source):
        return lax.dot_general(
            left, hots[source], (((1,), (1,)), ((), ())), preferred_element_type=F32
        )

    def count_tile(source, counts):
        return counts + product(jnp.where(row_hot_of(source), 1.0, 0.0).astype(BF16), source)

    counts = lax.fori_loop(0, tiles, count_tile, jnp.zeros((ocean_rows, columns), F32))

    def add_tile(source, acc):
        stress = cells[source]
        row_hot = row_hot_of(source)
        highs, lows = [], []
        for k in range(3):
            high, low = split_bf16(stress[k * rows : (k + 1) * rows])
            for value, into in ((high, highs), (low, lows)):
                value = lanes_of(value.astype(F32))
                into.append(jnp.where(row_hot, value, 0.0).astype(BF16))
        return acc + product(jnp.concatenate(highs + lows, axis=0), source)

    acc = add_tile(tile, jnp.zeros((6 * ocean_rows, columns), F32))

    def add_other(k, acc):
        source = lax.rem(tile + tiles - k, tiles)
        cell_copy(k, source).wait_recv()
        return add_tile(source, acc)

    acc = lax.fori_loop(1, tiles, add_other, acc)
    counts = jnp.maximum(counts, 1.0)
    for k in range(3):
        high = acc[k * ocean_rows : (k + 1) * ocean_rows]
        low = acc[(3 + k) * ocean_rows : (4 + k) * ocean_rows]
        mean = (high + low) / counts
        for r in range(ocean_rows):
            stress_ref[pl.ds(k, 1), pl.ds(r * columns, columns)] = mean[r : r + 1]

    for store in stores:
        store.wait()
    for c in range(CHUNKS):

        @pl.when(has_down)
        def _():
            halo_copy(0, c).wait_send()

        @pl.when(has_up)
        def _():
            halo_copy(1, c).wait_send()

    for k in range(1, sects):
        part_copy(k, sect).wait_send()

    @pl.loop(1, tiles)
    def _(k):
        table_copy(k, tile).wait_send()
        cell_copy(k, tile).wait_send()


def local(
    spectrum, courant, group_ratio, ocean_currents, elevation, sea_mask, owner_tile, ocean_slot
):
    bins, rows, columns = spectrum.shape
    tiles = lax.axis_size("tile")
    sects = lax.axis_size("sect")
    ocean_rows = elevation.shape[0] // columns
    angles = (np.arange(NDIR) + 0.5) * (2.0 * math.pi / NDIR)
    lines = -(-bins // GROUP) * GROUP
    extent = 2 * rows
    vmem = pl.BlockSpec(memory_space=pltpu.VMEM)
    hbm = pl.BlockSpec(memory_space=pltpu.HBM)
    dma = pltpu.SemaphoreType.DMA
    return pl.pallas_call(
        functools.partial(kernel, tiles, sects),
        out_shape=(
            jax.ShapeDtypeStruct(spectrum.shape, F32),
            jax.ShapeDtypeStruct((3, elevation.shape[0]), F32),
        ),
        in_specs=[hbm] * 9,
        out_specs=(hbm, vmem),
        scratch_shapes=[
            pltpu.SMEM((2 * NDIR + 8,), F32),
            pltpu.SMEM((NFREQ,), F32),
            pltpu.SMEM((NFREQ,), F32),
            pltpu.VMEM(ocean_currents.shape, F32),
            pltpu.VMEM((rows, columns), jnp.int32),
            pltpu.VMEM((rows, columns), jnp.int32),
            pltpu.VMEM((rows, columns), jnp.int32),
            pltpu.VMEM((tiles, 3 * ocean_rows + 2 * rows, columns), F32),
            pltpu.VMEM((lines, rows, columns), F32),
            pltpu.VMEM((lines, rows, columns), F32),
            pltpu.VMEM((lines, rows, columns), F32),
            pltpu.VMEM((3, rows, 2 * columns), F32),
            pltpu.VMEM((4, extent, GROUP, columns), F32),
            pltpu.VMEM((5, lines, columns), F32),
            pltpu.VMEM((2, NFREQ, columns), F32),
            pltpu.VMEM((tiles, columns, rows * columns), BF16),
            pltpu.VMEM((3, rows, GROUP, columns), F32),
            pltpu.VMEM((sects, 3 * rows, columns), F32),
            pltpu.VMEM((tiles, 3 * rows, columns), F32),
            dma((8,)),
            dma,
            dma((CHUNKS,)),
            dma((2, CHUNKS)),
            dma((2, CHUNKS)),
            dma((tiles,)),
            dma((tiles,)),
            dma((sects,)),
            dma((sects,)),
            dma((tiles,)),
            dma((tiles,)),
        ],
        compiler_params=pltpu.CompilerParams(
            collective_id=0, has_side_effects=True, vmem_limit_bytes=60 * 1024 * 1024
        ),
        cost_estimate=pl.CostEstimate(
            flops=bins * rows * columns * 200, bytes_accessed=8 * bins * rows * columns,
            transcendentals=0,
        ),
        name="coupling",
    )(
        jnp.asarray(np.concatenate([np.cos(angles), np.sin(angles), np.zeros(8)]), F32),
        courant,
        group_ratio,
        ocean_currents,
        elevation.reshape(ocean_rows, columns),
        sea_mask,
        owner_tile.reshape(rows, columns),
        ocean_slot.reshape(rows, columns),
        spectrum,
    )


def solution(mesh):
    in_specs = (
        P("sect", "tile", None),
        P(),
        P(),
        P(None, "tile"),
        P("tile"),
        P("tile", None),
        P("tile", None),
        P("tile"),
    )
    out_specs = (P("sect", "tile", None), P(None, "tile"))
    return jax.shard_map(local, mesh=mesh, in_specs=in_specs, out_specs=out_specs, check_vma=False)
```

```python
import functools
import math

import jax
import jax.numpy as jnp
import numpy as np
from jax import lax
from jax.experimental import pallas as pl
from jax.experimental.pallas import tpu as pltpu
from jax.sharding import PartitionSpec as P

NDIR = 36
NFREQ = 36
STEPS = 4
CHUNKS = 8
SHARES = (0, 6, 12, 18, 24, 30, 35, 39, 41)
GROUP = 8
MESH = pl.DeviceIdType.MESH
F32 = jnp.float32
BF16 = jnp.bfloat16


def split_bf16(x):
    high = x.astype(BF16)
    return high, (x - high.astype(F32)).astype(BF16)


def lanes_of(x):
    return jnp.concatenate([x[j : j + 1] for j in range(x.shape[0])], axis=1)


def chunk_bounds(groups):
    return [groups * share // SHARES[-1] for share in SHARES]


def kernel(
    tiles,
    sects,
    trig_hbm,
    courant_hbm,
    ratio_hbm,
    current_hbm,
    elevation_hbm,
    mask_hbm,
    owner_hbm,
    slot_hbm,
    spectrum_ref,
    out_ref,
    stress_ref,
    trig_ref,
    courant_ref,
    ratio_ref,
    current_ref,
    mask_ref,
    owner_ref,
    slot_ref,
    bundle,
    table,
    energy,
    packed,
    result,
    halo,
    flow,
    fields,
    scalars,
    by_freq,
    hots,
    sums,
    parts,
    cells,
    small_sem,
    load_sem,
    out_sem,
    halo_send,
    halo_recv,
    table_send,
    table_recv,
    forward_send,
    forward_recv,
    part_send,
    part_recv,
    cell_send,
    cell_recv,
):
    tile = lax.axis_index("tile")
    sect = lax.axis_index("sect")
    bins = spectrum_ref.shape[0]
    rows, columns = mask_ref.shape
    half = rows // 2
    ocean_rows = elevation_hbm.shape[0]
    ocean_cells = ocean_rows * columns
    groups = halo.shape[1] // GROUP
    bounds = chunk_bounds(groups)
    first = 3 * ocean_rows
    shift = columns.bit_length() - 1
    has_up = tile < tiles - 1
    has_down = tile > 0
    up = lax.rem(tile + 1, tiles)
    down = lax.rem(tile + tiles - 1, tiles)

    load = pltpu.make_async_copy(spectrum_ref, energy.at[pl.ds(0, bins)], load_sem)
    load.start()

    small = [
        (trig_hbm, trig_ref),
        (courant_hbm, courant_ref),
        (ratio_hbm, ratio_ref),
        (current_hbm, current_ref),
        (elevation_hbm, bundle.at[pl.ds(2 * ocean_rows, ocean_rows)]),
        (mask_hbm, mask_ref),
        (owner_hbm, owner_ref),
        (slot_hbm, slot_ref),
    ]
    small = [pltpu.make_async_copy(a, b, small_sem.at[i]) for i, (a, b) in enumerate(small)]
    for copy in small:
        copy.start()
    barrier = pltpu.get_barrier_semaphore()

    @pl.loop(1, tiles)
    def _(k):
        pl.semaphore_signal(
            barrier, inc=1, device_id=(sect, lax.rem(tile + k, tiles)), device_id_type=MESH
        )

    @pl.loop(1, sects)
    def _(k):
        pl.semaphore_signal(
            barrier, inc=1, device_id=(lax.rem(sect + k, sects), tile), device_id_type=MESH
        )

    lines = groups * GROUP
    spare = lines - bins
    energy_rows = energy.reshape(lines * rows, columns)
    result_rows = result.reshape(lines * rows, columns)
    for b in range(bins, lines):
        energy[b] = jnp.zeros((rows, columns), F32)

    def pack(g, _):
        for r in range(rows):
            packed[r, pl.ds(g * GROUP, GROUP), :] = energy_rows[
                pl.ds(g * GROUP * rows + r, GROUP, stride=rows), :
            ]
        return 0

    def halo_copy(side, c):
        begin, end = bounds[c] * GROUP, bounds[c + 1] * GROUP
        at = (pl.ds(side * half, half), pl.ds(begin, end - begin))
        return pltpu.make_async_remote_copy(
            src_ref=packed.at[at],
            dst_ref=halo.at[at],
            send_sem=halo_send.at[side, c],
            recv_sem=halo_recv.at[side, c],
            device_id=(sect, down if side == 0 else up),
            device_id_type=MESH,
        )

    def send_chunk(c):
        @pl.when(has_down)
        def _():
            halo_copy(0, c).start()

        @pl.when(has_up)
        def _():
            halo_copy(1, c).start()

    load.wait()
    lax.fori_loop(bounds[0], bounds[1], pack, 0)
    pl.semaphore_wait(barrier, tiles + sects - 2)
    send_chunk(0)

    for copy in small:
        copy.wait()
    for r in range(ocean_rows):
        at = pl.ds(r * columns, columns)
        bundle[pl.ds(r, 1), :] = current_ref[pl.ds(0, 1), at]
        bundle[pl.ds(ocean_rows + r, 1), :] = current_ref[pl.ds(1, 1), at]
    bundle[pl.ds(first, rows), :] = (owner_ref[...] * ocean_cells + slot_ref[...]).astype(F32)
    bundle[pl.ds(first + rows, rows), :] = mask_ref[...].astype(F32)
    share = bundle.shape[0] // sects
    piece = pl.ds(pl.multiple_of(sect * share, 8), share)
    table[tile, piece, :] = bundle[piece, :]

    def table_copy(k, slot):
        return pltpu.make_async_remote_copy(
            src_ref=bundle.at[piece],
            dst_ref=table.at[slot, piece],
            send_sem=table_send.at[k],
            recv_sem=table_recv.at[slot],
            device_id=(sect, lax.rem(tile + k, tiles)),
            device_id_type=MESH,
        )

    def forward_copy(k, source):
        at = pl.ds(pl.multiple_of(source * share, 8), share)
        return pltpu.make_async_remote_copy(
            src_ref=table.at[:, at],
            dst_ref=table.at[:, at],
            send_sem=forward_send.at[k],
            recv_sem=forward_recv.at[source],
            device_id=(lax.rem(sect + k, sects), tile),
            device_id_type=MESH,
        )

    @pl.loop(1, tiles)
    def _(k):
        table_copy(k, tile).start()

    for c in range(1, CHUNKS):
        lax.fori_loop(bounds[c], bounds[c + 1], pack, 0)
        send_chunk(c)

    start = sect * bins
    first_dir, first_freq = start // NFREQ, start % NFREQ
    for i in range(NFREQ):
        f = first_freq + i
        f = jnp.where(f >= NFREQ, f - NFREQ, f)
        by_freq[0, pl.ds(i, 1), :] = jnp.full((1, columns), courant_ref[f], F32)
        by_freq[1, pl.ds(i, 1), :] = jnp.full((1, columns), ratio_ref[f], F32)
    speed, ratio = by_freq[0], by_freq[1]
    wrapped = lax.broadcasted_iota(jnp.int32, (NFREQ, columns), 0) + first_freq >= NFREQ
    scale = 4.0 / (NDIR * NFREQ)
    for begin in range(0, bins, NFREQ):
        count = min(NFREQ, bins - begin)
        d = first_dir + begin // NFREQ
        c = jnp.where(wrapped, trig_ref[d + 1], trig_ref[d])
        s = jnp.where(wrapped, trig_ref[NDIR + d + 1], trig_ref[NDIR + d])
        values = (
            speed * c,
            speed * s,
            (ratio * (1.0 + c * c) - 0.5) * scale,
            (ratio * c * s) * scale,
            (ratio * (1.0 + s * s) - 0.5) * scale,
        )
        for q in range(5):
            scalars[q, pl.ds(begin, count), :] = values[q][:count]
    if spare:
        for q in range(5):
            scalars[q, pl.ds(bins, spare), :] = jnp.zeros((spare, columns), F32)
    sums[...] = jnp.zeros_like(sums)

    @pl.loop(1, tiles)
    def _(k):
        table_copy(k, lax.rem(tile + tiles - k, tiles)).wait_recv()

    for k in range(1, sects):
        forward_copy(k, sect).start()
    for k in range(1, sects):
        forward_copy(k, lax.rem(sect + sects - k, sects)).wait_recv()

    sub = lax.broadcasted_iota(jnp.int32, (rows, columns), 0)
    upper = sub < half
    valid = (upper & has_up) | (jnp.logical_not(upper) & has_down)

    def ring(start):
        own = table[tile, pl.ds(start, rows), :]
        other = jnp.where(
            upper, table[up, pl.ds(start, rows), :], table[down, pl.ds(start, rows), :]
        )
        return own, other

    target_own, target_halo = ring(first)
    mask_own, mask_halo = ring(first + rows)
    mask_halo = jnp.where(valid, mask_halo, 0.0)
    target_own = target_own.astype(jnp.int32)
    target_halo = target_halo.astype(jnp.int32)

    table_rows = tiles * ocean_rows
    pieces = []
    for field in range(3):
        whole = table[:, pl.ds(field * ocean_rows, ocean_rows), :].reshape(table_rows, columns)
        high, low = split_bf16(whole.T)
        pieces.append(jnp.concatenate([high, low], axis=1))
    lookup = jnp.concatenate(pieces, axis=0)
    row_ids = lax.broadcasted_iota(jnp.int32, (table_rows, 2 * columns), 0)
    lane_ids = lax.broadcasted_iota(jnp.int32, (columns, 2 * columns), 0)
    for j in range(rows):
        index = jnp.concatenate([target_own[j : j + 1], target_halo[j : j + 1]], axis=1)
        hot = jnp.where(row_ids == index >> shift, 1.0, 0.0).astype(BF16)
        found = jnp.dot(
            lookup, jnp.concatenate([hot, hot], axis=0), preferred_element_type=F32
        )
        chosen = lane_ids == (index & (columns - 1))
        for field in range(3):
            value = jnp.sum(
                jnp.where(chosen, found[field * columns : (field + 1) * columns], 0.0),
                axis=0,
                keepdims=True,
            )
            flow[field, pl.ds(j, 1), :] = value

    def east(x):
        return pltpu.roll(x, columns - 1, 1)

    def west(x):
        return pltpu.roll(x, 1, 1)

    u_own = flow[0, :, pl.ds(0, columns)]
    u_halo = jnp.where(valid, flow[0, :, pl.ds(columns, columns)], 0.0)
    v_own = flow[1, :, pl.ds(0, columns)]
    v_halo = jnp.where(valid, flow[1, :, pl.ds(columns, columns)], 0.0)
    factor = (1.0 + flow[2, :, pl.ds(0, columns)]) * mask_own
    extent = rows + 2 * half

    def in_order(own, other):
        return jnp.concatenate([other[half:], own, other[:half]], axis=0)

    u_all = in_order(u_own, u_halo)
    v_all = in_order(v_own, v_halo)
    m_all = in_order(mask_own, mask_halo)
    ux_all = 0.5 * (u_all + east(u_all))
    uw_all = west(ux_all)
    vy_all = 0.5 * (v_all[:-1] + v_all[1:])
    for j in range(extent):
        fields[0, j] = jnp.broadcast_to(ux_all[j : j + 1], (GROUP, columns))
        fields[1, j] = jnp.broadcast_to(uw_all[j : j + 1], (GROUP, columns))
        fields[2, j] = jnp.broadcast_to(m_all[j : j + 1], (GROUP, columns))
        if j < extent - 1:
            fields[3, j] = jnp.broadcast_to(vy_all[j : j + 1], (GROUP, columns))

    def one_group(g, _):
        begin = g * GROUP
        base = begin * rows
        e = {}
        for j in range(rows):
            e[half + j] = packed[j, pl.ds(begin, GROUP), :]
            outside = halo[j, pl.ds(begin, GROUP), :]
            if j < half:
                e[half + rows + j] = jnp.where(has_up, outside, 0.0)
            else:
                e[j - half] = jnp.where(has_down, outside, 0.0)
        sx = scalars[0, pl.ds(begin, GROUP), :]
        sy = scalars[1, pl.ds(begin, GROUP), :]
        yp, ym, xm, xpw, c0 = {}, {}, {}, {}, {}

        def coefficients(j):
            ay = sy + fields[3, j]
            yp[j], ym[j] = jnp.maximum(ay, 0.0), jnp.minimum(ay, 0.0)
            if j:
                ax = sx + fields[0, j]
                aw = sx + fields[1, j]
                xm[j] = jnp.minimum(ax, 0.0)
                xpw[j] = jnp.maximum(aw, 0.0)
                c0[j] = (1.0 - jnp.maximum(ax, 0.0) + jnp.minimum(aw, 0.0)) - (yp[j] - ym[j - 1])

        levels = [e] + [{} for _ in range(STEPS)]
        coefficients(0)
        for wave in range(1, extent + 2 * STEPS):
            if wave < extent - 1:
                coefficients(wave)
            for step in range(STEPS, 0, -1):
                j = wave - 2 * (step - 1)
                if step <= j < extent - step:
                    old = levels[step - 1]
                    value = c0[j] * old[j] - xm[j] * east(old[j]) + xpw[j] * west(old[j])
                    value = value - ym[j] * old[j + 1] + yp[j - 1] * old[j - 1]
                    levels[step][j] = fields[2, j] * value
        e = levels[STEPS]
        weights = [scalars[2 + k, pl.ds(begin, GROUP), :] for k in range(3)]
        for j in range(rows):
            final = e[half + j]
            result_rows[pl.ds(base + j, GROUP, stride=rows), :] = final
            for k in range(3):
                sums[k, j] += weights[k] * final
        return 0

    stores = []
    for c in range(CHUNKS):

        @pl.when(has_up)
        def _():
            halo_copy(0, c).wait_recv()

        @pl.when(has_down)
        def _():
            halo_copy(1, c).wait_recv()

        lax.fori_loop(bounds[c], bounds[c + 1], one_group, 0)
        begin, end = bounds[c] * GROUP, min(bounds[c + 1] * GROUP, bins)
        at = pl.ds(begin, end - begin)
        store = pltpu.make_async_copy(result.at[at], out_ref.at[at], out_sem.at[c])
        store.start()
        stores.append(store)

    def part_copy(k, slot):
        return pltpu.make_async_remote_copy(
            src_ref=parts.at[sect],
            dst_ref=parts.at[slot],
            send_sem=part_send.at[k],
            recv_sem=part_recv.at[slot],
            device_id=(lax.rem(sect + k, sects), tile),
            device_id_type=MESH,
        )

    for k in range(3):
        for j in range(rows):
            parts[sect, pl.ds(k * rows + j, 1), :] = jnp.sum(sums[k, j], axis=0, keepdims=True)
    for k in range(1, sects):
        part_copy(k, sect).start()

    cell_count = rows * columns
    ocean_ids = lax.broadcasted_iota(jnp.int32, (ocean_rows, cell_count), 0) + tile * ocean_rows

    def index_of(source):
        return lanes_of(table[source, pl.ds(first, rows), :].astype(jnp.int32))

    def row_hot_of(source):
        return ocean_ids == index_of(source) >> shift

    @pl.loop(0, tiles)
    def _(source):
        lane = index_of(source) & (columns - 1)
        ids = lax.broadcasted_iota(jnp.int32, (columns, cell_count), 0)
        hots[source] = jnp.where(ids == lane, 1.0, 0.0).astype(BF16)

    for k in range(1, sects):
        part_copy(k, lax.rem(sect + sects - k, sects)).wait_recv()
    total = parts[0]
    for k in range(1, sects):
        total = total + parts[k]
    cells[tile] = total * jnp.concatenate([factor] * 3, axis=0)

    def cell_copy(k, slot):
        return pltpu.make_async_remote_copy(
            src_ref=cells.at[tile],
            dst_ref=cells.at[slot],
            send_sem=cell_send.at[k],
            recv_sem=cell_recv.at[slot],
            device_id=(sect, lax.rem(tile + k, tiles)),
            device_id_type=MESH,
        )

    @pl.loop(1, tiles)
    def _(k):
        cell_copy(k, tile).start()

    def product(left, source):
        return lax.dot_general(
            left, hots[source], (((1,), (1,)), ((), ())), preferred_element_type=F32
        )

    def count_tile(source, counts):
        return counts + product(jnp.where(row_hot_of(source), 1.0, 0.0).astype(BF16), source)

    counts = lax.fori_loop(0, tiles, count_tile, jnp.zeros((ocean_rows, columns), F32))

    def add_tile(source, acc):
        stress = cells[source]
        row_hot = row_hot_of(source)
        highs, lows = [], []
        for k in range(3):
            high, low = split_bf16(stress[k * rows : (k + 1) * rows])
            for value, into in ((high, highs), (low, lows)):
                value = lanes_of(value.astype(F32))
                into.append(jnp.where(row_hot, value, 0.0).astype(BF16))
        return acc + product(jnp.concatenate(highs + lows, axis=0), source)

    acc = add_tile(tile, jnp.zeros((6 * ocean_rows, columns), F32))

    def add_other(k, acc):
        source = lax.rem(tile + tiles - k, tiles)
        cell_copy(k, source).wait_recv()
        return add_tile(source, acc)

    acc = lax.fori_loop(1, tiles, add_other, acc)
    counts = jnp.maximum(counts, 1.0)
    for k in range(3):
        high = acc[k * ocean_rows : (k + 1) * ocean_rows]
        low = acc[(3 + k) * ocean_rows : (4 + k) * ocean_rows]
        mean = (high + low) / counts
        for r in range(ocean_rows):
            stress_ref[pl.ds(k, 1), pl.ds(r * columns, columns)] = mean[r : r + 1]

    for store in stores:
        store.wait()
    for c in range(CHUNKS):

        @pl.when(has_down)
        def _():
            halo_copy(0, c).wait_send()

        @pl.when(has_up)
        def _():
            halo_copy(1, c).wait_send()

    for k in range(1, sects):
        part_copy(k, sect).wait_send()

    for k in range(1, sects):
        forward_copy(k, sect).wait_send()

    @pl.loop(1, tiles)
    def _(k):
        table_copy(k, tile).wait_send()
        cell_copy(k, tile).wait_send()


def local(
    spectrum, courant, group_ratio, ocean_currents, elevation, sea_mask, owner_tile, ocean_slot
):
    bins, rows, columns = spectrum.shape
    tiles = lax.axis_size("tile")
    sects = lax.axis_size("sect")
    ocean_rows = elevation.shape[0] // columns
    angles = (np.arange(NDIR) + 0.5) * (2.0 * math.pi / NDIR)
    lines = -(-bins // GROUP) * GROUP
    extent = 2 * rows
    vmem = pl.BlockSpec(memory_space=pltpu.VMEM)
    hbm = pl.BlockSpec(memory_space=pltpu.HBM)
    dma = pltpu.SemaphoreType.DMA
    return pl.pallas_call(
        functools.partial(kernel, tiles, sects),
        out_shape=(
            jax.ShapeDtypeStruct(spectrum.shape, F32),
            jax.ShapeDtypeStruct((3, elevation.shape[0]), F32),
        ),
        in_specs=[hbm] * 9,
        out_specs=(hbm, vmem),
        scratch_shapes=[
            pltpu.SMEM((2 * NDIR + 8,), F32),
            pltpu.SMEM((NFREQ,), F32),
            pltpu.SMEM((NFREQ,), F32),
            pltpu.VMEM(ocean_currents.shape, F32),
            pltpu.VMEM((rows, columns), jnp.int32),
            pltpu.VMEM((rows, columns), jnp.int32),
            pltpu.VMEM((rows, columns), jnp.int32),
            pltpu.VMEM((3 * ocean_rows + 2 * rows, columns), F32),
            pltpu.VMEM((tiles, 3 * ocean_rows + 2 * rows, columns), F32),
            pltpu.VMEM((lines, rows, columns), F32),
            pltpu.VMEM((rows, lines, columns), F32),
            pltpu.VMEM((lines, rows, columns), F32),
            pltpu.VMEM((rows, lines, columns), F32),
            pltpu.VMEM((3, rows, 2 * columns), F32),
            pltpu.VMEM((4, extent, GROUP, columns), F32),
            pltpu.VMEM((5, lines, columns), F32),
            pltpu.VMEM((2, NFREQ, columns), F32),
            pltpu.VMEM((tiles, columns, rows * columns), BF16),
            pltpu.VMEM((3, rows, GROUP, columns), F32),
            pltpu.VMEM((sects, 3 * rows, columns), F32),
            pltpu.VMEM((tiles, 3 * rows, columns), F32),
            dma((8,)),
            dma,
            dma((CHUNKS,)),
            dma((2, CHUNKS)),
            dma((2, CHUNKS)),
            dma((tiles,)),
            dma((tiles,)),
            dma((sects,)),
            dma((sects,)),
            dma((sects,)),
            dma((sects,)),
            dma((tiles,)),
            dma((tiles,)),
        ],
        compiler_params=pltpu.CompilerParams(
            collective_id=0, has_side_effects=True, vmem_limit_bytes=60 * 1024 * 1024
        ),
        cost_estimate=pl.CostEstimate(
            flops=bins * rows * columns * 200, bytes_accessed=8 * bins * rows * columns,
            transcendentals=0,
        ),
        name="coupling",
    )(
        jnp.asarray(np.concatenate([np.cos(angles), np.sin(angles), np.zeros(8)]), F32),
        courant,
        group_ratio,
        ocean_currents,
        elevation.reshape(ocean_rows, columns),
        sea_mask,
        owner_tile.reshape(rows, columns),
        ocean_slot.reshape(rows, columns),
        spectrum,
    )


def solution(mesh):
    in_specs = (
        P("sect", "tile", None),
        P(),
        P(),
        P(None, "tile"),
        P("tile"),
        P("tile", None),
        P("tile", None),
        P("tile"),
    )
    out_specs = (P("sect", "tile", None), P(None, "tile"))
    return jax.shard_map(local, mesh=mesh, in_specs=in_specs, out_specs=out_specs, check_vma=False)
```

```python
import functools
import math

import jax
import jax.numpy as jnp
import numpy as np
from jax import lax
from jax.experimental import pallas as pl
from jax.experimental.pallas import tpu as pltpu
from jax.sharding import PartitionSpec as P

NDIR = 36
NFREQ = 36
STEPS = 4
CHUNKS = 7
ABREAST = 3
GROUP = 8
MESH = pl.DeviceIdType.MESH
F32 = jnp.float32
BF16 = jnp.bfloat16


def split_bf16(x):
    high = x.astype(BF16)
    return high, (x - high.astype(F32)).astype(BF16)


def lanes_of(x):
    return jnp.concatenate([x[j : j + 1] for j in range(x.shape[0])], axis=1)


def kernel(
    tiles,
    sects,
    trig_hbm,
    courant_hbm,
    ratio_hbm,
    current_hbm,
    elevation_hbm,
    mask_hbm,
    owner_hbm,
    slot_hbm,
    spectrum_ref,
    out_ref,
    stress_ref,
    trig_ref,
    courant_ref,
    ratio_ref,
    current_ref,
    mask_ref,
    owner_ref,
    slot_ref,
    bundle,
    table,
    energy,
    packed,
    result,
    halo,
    flow,
    fields,
    scalars,
    by_freq,
    hots,
    sums,
    parts,
    cells,
    small_sem,
    load_sem,
    out_sem,
    halo_send,
    halo_recv,
    table_send,
    table_recv,
    part_send,
    part_recv,
    cell_send,
    cell_recv,
):
    tile = lax.axis_index("tile")
    sect = lax.axis_index("sect")
    bins = spectrum_ref.shape[0]
    rows, columns = mask_ref.shape
    half = rows // 2
    ocean_rows = elevation_hbm.shape[0]
    ocean_cells = ocean_rows * columns
    lines = halo.shape[1]
    per = lines // CHUNKS
    first = 3 * ocean_rows
    shift = columns.bit_length() - 1
    has_up = tile < tiles - 1
    has_down = tile > 0
    up = lax.rem(tile + 1, tiles)
    down = lax.rem(tile + tiles - 1, tiles)

    load = pltpu.make_async_copy(spectrum_ref, energy.at[pl.ds(0, bins)], load_sem)
    load.start()

    small = [
        (trig_hbm, trig_ref),
        (courant_hbm, courant_ref),
        (ratio_hbm, ratio_ref),
        (current_hbm, current_ref),
        (elevation_hbm, bundle.at[pl.ds(2 * ocean_rows, ocean_rows)]),
        (mask_hbm, mask_ref),
        (owner_hbm, owner_ref),
        (slot_hbm, slot_ref),
    ]
    small = [pltpu.make_async_copy(a, b, small_sem.at[i]) for i, (a, b) in enumerate(small)]
    for copy in small:
        copy.start()
    barrier = pltpu.get_barrier_semaphore()

    @pl.loop(1, tiles)
    def _(k):
        pl.semaphore_signal(
            barrier, inc=1, device_id=(sect, lax.rem(tile + k, tiles)), device_id_type=MESH
        )

    @pl.loop(1, sects)
    def _(k):
        pl.semaphore_signal(
            barrier, inc=1, device_id=(lax.rem(sect + k, sects), tile), device_id_type=MESH
        )

    spare = lines - bins
    energy_rows = energy.reshape(lines * rows, columns)
    result_rows = result.reshape(lines * rows, columns)
    for b in range(bins, lines):
        energy[b] = jnp.zeros((rows, columns), F32)

    def pack(g):
        for r in range(rows):
            packed[r, pl.ds(pl.multiple_of(g * GROUP, GROUP), GROUP), :] = energy_rows[
                pl.ds(g * GROUP * rows + r, GROUP, stride=rows), :
            ]

    def halo_copy(side, c):
        at = (pl.ds(side * half, half), pl.ds(pl.multiple_of(c * per, GROUP), per))
        return pltpu.make_async_remote_copy(
            src_ref=packed.at[at],
            dst_ref=halo.at[at],
            send_sem=halo_send.at[side, c],
            recv_sem=halo_recv.at[side, c],
            device_id=(sect, down if side == 0 else up),
            device_id_type=MESH,
        )

    for copy in small:
        copy.wait()
    for r in range(ocean_rows):
        at = pl.ds(r * columns, columns)
        bundle[pl.ds(r, 1), :] = current_ref[pl.ds(0, 1), at]
        bundle[pl.ds(ocean_rows + r, 1), :] = current_ref[pl.ds(1, 1), at]
    bundle[pl.ds(first, rows), :] = (owner_ref[...] * ocean_cells + slot_ref[...]).astype(F32)
    bundle[pl.ds(first + rows, rows), :] = mask_ref[...].astype(F32)
    table[tile] = bundle[...]
    pl.semaphore_wait(barrier, tiles + sects - 2)

    def table_copy(k, slot):
        return pltpu.make_async_remote_copy(
            src_ref=bundle,
            dst_ref=table.at[slot],
            send_sem=table_send.at[k],
            recv_sem=table_recv.at[slot],
            device_id=(sect, lax.rem(tile + k, tiles)),
            device_id_type=MESH,
        )

    @pl.loop(1, tiles)
    def _(k):
        table_copy(k, tile).start()

    load.wait()

    @pl.loop(0, CHUNKS)
    def _(c):
        for g in range(per // GROUP):
            pack(c * (per // GROUP) + g)

        @pl.when(has_down)
        def _():
            halo_copy(0, c).start()

        @pl.when(has_up)
        def _():
            halo_copy(1, c).start()

    @pl.when(jnp.logical_not(has_up))
    def _():
        halo[pl.ds(0, half)] = jnp.zeros((half, lines, columns), F32)

    @pl.when(jnp.logical_not(has_down))
    def _():
        halo[pl.ds(half, half)] = jnp.zeros((half, lines, columns), F32)

    start = sect * bins
    first_dir, first_freq = start // NFREQ, start % NFREQ
    for i in range(NFREQ):
        f = first_freq + i
        f = jnp.where(f >= NFREQ, f - NFREQ, f)
        by_freq[0, pl.ds(i, 1), :] = jnp.full((1, columns), courant_ref[f], F32)
        by_freq[1, pl.ds(i, 1), :] = jnp.full((1, columns), ratio_ref[f], F32)
    speed, ratio = by_freq[0], by_freq[1]
    wrapped = lax.broadcasted_iota(jnp.int32, (NFREQ, columns), 0) + first_freq >= NFREQ
    scale = 4.0 / (NDIR * NFREQ)
    for begin in range(0, bins, NFREQ):
        count = min(NFREQ, bins - begin)
        d = first_dir + begin // NFREQ
        c = jnp.where(wrapped, trig_ref[d + 1], trig_ref[d])
        s = jnp.where(wrapped, trig_ref[NDIR + d + 1], trig_ref[NDIR + d])
        values = (
            speed * c,
            speed * s,
            (ratio * (1.0 + c * c) - 0.5) * scale,
            (ratio * c * s) * scale,
            (ratio * (1.0 + s * s) - 0.5) * scale,
        )
        for q in range(5):
            scalars[q, pl.ds(begin, count), :] = values[q][:count]
    if spare:
        for q in range(5):
            scalars[q, pl.ds(bins, spare), :] = jnp.zeros((spare, columns), F32)
    sums[...] = jnp.zeros_like(sums)

    @pl.loop(1, tiles)
    def _(k):
        table_copy(k, lax.rem(tile + tiles - k, tiles)).wait_recv()

    sub = lax.broadcasted_iota(jnp.int32, (rows, columns), 0)
    upper = sub < half
    valid = (upper & has_up) | (jnp.logical_not(upper) & has_down)

    def ring(start):
        own = table[tile, pl.ds(start, rows), :]
        other = jnp.where(
            upper, table[up, pl.ds(start, rows), :], table[down, pl.ds(start, rows), :]
        )
        return own, other

    target_own, target_halo = ring(first)
    mask_own, mask_halo = ring(first + rows)
    mask_halo = jnp.where(valid, mask_halo, 0.0)
    target_own = target_own.astype(jnp.int32)
    target_halo = target_halo.astype(jnp.int32)

    table_rows = tiles * ocean_rows
    pieces = []
    for field in range(3):
        whole = table[:, pl.ds(field * ocean_rows, ocean_rows), :].reshape(table_rows, columns)
        high, low = split_bf16(whole.T)
        pieces.append(jnp.concatenate([high, low], axis=1))
    lookup = jnp.concatenate(pieces, axis=0)
    row_ids = lax.broadcasted_iota(jnp.int32, (table_rows, 2 * columns), 0)
    lane_ids = lax.broadcasted_iota(jnp.int32, (columns, 2 * columns), 0)
    for j in range(rows):
        index = jnp.concatenate([target_own[j : j + 1], target_halo[j : j + 1]], axis=1)
        hot = jnp.where(row_ids == index >> shift, 1.0, 0.0).astype(BF16)
        found = jnp.dot(
            lookup, jnp.concatenate([hot, hot], axis=0), preferred_element_type=F32
        )
        chosen = lane_ids == (index & (columns - 1))
        for field in range(3):
            value = jnp.sum(
                jnp.where(chosen, found[field * columns : (field + 1) * columns], 0.0),
                axis=0,
                keepdims=True,
            )
            flow[field, pl.ds(j, 1), :] = value

    def east(x):
        return pltpu.roll(x, columns - 1, 1)

    def west(x):
        return pltpu.roll(x, 1, 1)

    u_own = flow[0, :, pl.ds(0, columns)]
    u_halo = jnp.where(valid, flow[0, :, pl.ds(columns, columns)], 0.0)
    v_own = flow[1, :, pl.ds(0, columns)]
    v_halo = jnp.where(valid, flow[1, :, pl.ds(columns, columns)], 0.0)
    factor = (1.0 + flow[2, :, pl.ds(0, columns)]) * mask_own
    extent = rows + 2 * half

    def in_order(own, other):
        return jnp.concatenate([other[half:], own, other[:half]], axis=0)

    u_all = in_order(u_own, u_halo)
    v_all = in_order(v_own, v_halo)
    m_all = in_order(mask_own, mask_halo)
    ux_all = 0.5 * (u_all + east(u_all))
    uw_all = west(ux_all)
    vy_all = 0.5 * (v_all[:-1] + v_all[1:])
    for j in range(extent):
        fields[0, j] = jnp.broadcast_to(ux_all[j : j + 1], (GROUP, columns))
        fields[1, j] = jnp.broadcast_to(uw_all[j : j + 1], (GROUP, columns))
        fields[2, j] = jnp.broadcast_to(m_all[j : j + 1], (GROUP, columns))
        if j < extent - 1:
            fields[3, j] = jnp.broadcast_to(vy_all[j : j + 1], (GROUP, columns))

    class Group:
        def __init__(self, begin):
            begin = pl.multiple_of(begin, GROUP)
            self.begin = begin
            self.yp, self.ym, self.xm, self.xpw, self.c0 = {}, {}, {}, {}, {}
            self.sx = scalars[0, pl.ds(begin, GROUP), :]
            self.sy = scalars[1, pl.ds(begin, GROUP), :]
            e = {}
            for j in range(rows):
                e[half + j] = packed[j, pl.ds(begin, GROUP), :]
                e[half + rows + j if j < half else j - half] = halo[j, pl.ds(begin, GROUP), :]
            self.levels = [e] + [{} for _ in range(STEPS)]

        def coefficients(self, j):
            ay = self.sy + fields[3, j]
            self.yp[j], self.ym[j] = jnp.maximum(ay, 0.0), jnp.minimum(ay, 0.0)
            if j:
                ax = self.sx + fields[0, j]
                aw = self.sx + fields[1, j]
                self.xm[j] = jnp.minimum(ax, 0.0)
                self.xpw[j] = jnp.maximum(aw, 0.0)
                out_x = jnp.maximum(ax, 0.0) - jnp.minimum(aw, 0.0)
                self.c0[j] = (1.0 - out_x) - (self.yp[j] - self.ym[j - 1])

        def advance(self, step, j):
            old = self.levels[step - 1]
            value = self.c0[j] * old[j] - self.xm[j] * east(old[j]) + self.xpw[j] * west(old[j])
            value = value - self.ym[j] * old[j + 1] + self.yp[j - 1] * old[j - 1]
            self.levels[step][j] = fields[2, j] * value

    def abreast(begin):
        members = [Group(begin + i * GROUP) for i in range(ABREAST)]
        for member in members:
            member.coefficients(0)
        for wave in range(1, extent + 2 * STEPS):
            for member in members:
                if wave < extent - 1:
                    member.coefficients(wave)
            for step in range(STEPS, 0, -1):
                j = wave - 2 * (step - 1)
                if step <= j < extent - step:
                    for member in members:
                        member.advance(step, j)
        for member in members:
            for j in range(rows):
                result_rows[pl.ds(member.begin * rows + j, GROUP, stride=rows), :] = (
                    member.levels[STEPS][half + j]
                )
        for k in range(3):
            weights = [scalars[2 + k, pl.ds(member.begin, GROUP), :] for member in members]
            for j in range(rows):
                added = sums[k, j]
                for member, weight in zip(members, weights):
                    added = added + weight * member.levels[STEPS][half + j]
                sums[k, j] = added

    @pl.loop(0, CHUNKS)
    def _(c):
        @pl.when(has_up)
        def _():
            halo_copy(0, c).wait_recv()

        @pl.when(has_down)
        def _():
            halo_copy(1, c).wait_recv()

        @pl.loop(0, per // (GROUP * ABREAST))
        def _(i):
            abreast(c * per + i * (GROUP * ABREAST))

    store = pltpu.make_async_copy(result.at[pl.ds(0, bins)], out_ref, out_sem)
    store.start()

    def part_copy(k, slot):
        return pltpu.make_async_remote_copy(
            src_ref=parts.at[sect],
            dst_ref=parts.at[slot],
            send_sem=part_send.at[k],
            recv_sem=part_recv.at[slot],
            device_id=(lax.rem(sect + k, sects), tile),
            device_id_type=MESH,
        )

    for k in range(3):
        for j in range(rows):
            parts[sect, pl.ds(k * rows + j, 1), :] = jnp.sum(sums[k, j], axis=0, keepdims=True)
    for k in range(1, sects):
        part_copy(k, sect).start()

    cell_count = rows * columns
    ocean_ids = lax.broadcasted_iota(jnp.int32, (ocean_rows, cell_count), 0) + tile * ocean_rows

    def index_of(source):
        return lanes_of(table[source, pl.ds(first, rows), :].astype(jnp.int32))

    def row_hot_of(source):
        return ocean_ids == index_of(source) >> shift

    @pl.loop(0, tiles)
    def _(source):
        lane = index_of(source) & (columns - 1)
        ids = lax.broadcasted_iota(jnp.int32, (columns, cell_count), 0)
        hots[source] = jnp.where(ids == lane, 1.0, 0.0).astype(BF16)

    for k in range(1, sects):
        part_copy(k, lax.rem(sect + sects - k, sects)).wait_recv()
    total = parts[0]
    for k in range(1, sects):
        total = total + parts[k]
    cells[tile] = total * jnp.concatenate([factor] * 3, axis=0)

    def cell_copy(k, slot):
        return pltpu.make_async_remote_copy(
            src_ref=cells.at[tile],
            dst_ref=cells.at[slot],
            send_sem=cell_send.at[k],
            recv_sem=cell_recv.at[slot],
            device_id=(sect, lax.rem(tile + k, tiles)),
            device_id_type=MESH,
        )

    @pl.loop(1, tiles)
    def _(k):
        cell_copy(k, tile).start()

    def product(left, source):
        return lax.dot_general(
            left, hots[source], (((1,), (1,)), ((), ())), preferred_element_type=F32
        )

    def count_tile(source, counts):
        return counts + product(jnp.where(row_hot_of(source), 1.0, 0.0).astype(BF16), source)

    counts = lax.fori_loop(0, tiles, count_tile, jnp.zeros((ocean_rows, columns), F32))

    def add_tile(source, acc):
        stress = cells[source]
        row_hot = row_hot_of(source)
        highs, lows = [], []
        for k in range(3):
            high, low = split_bf16(stress[k * rows : (k + 1) * rows])
            for value, into in ((high, highs), (low, lows)):
                value = lanes_of(value.astype(F32))
                into.append(jnp.where(row_hot, value, 0.0).astype(BF16))
        return acc + product(jnp.concatenate(highs + lows, axis=0), source)

    acc = add_tile(tile, jnp.zeros((6 * ocean_rows, columns), F32))

    def add_other(k, acc):
        source = lax.rem(tile + tiles - k, tiles)
        cell_copy(k, source).wait_recv()
        return add_tile(source, acc)

    acc = lax.fori_loop(1, tiles, add_other, acc)
    counts = jnp.maximum(counts, 1.0)
    for k in range(3):
        high = acc[k * ocean_rows : (k + 1) * ocean_rows]
        low = acc[(3 + k) * ocean_rows : (4 + k) * ocean_rows]
        mean = (high + low) / counts
        for r in range(ocean_rows):
            stress_ref[pl.ds(k, 1), pl.ds(r * columns, columns)] = mean[r : r + 1]

    store.wait()
    for c in range(CHUNKS):

        @pl.when(has_down)
        def _():
            halo_copy(0, c).wait_send()

        @pl.when(has_up)
        def _():
            halo_copy(1, c).wait_send()

    for k in range(1, sects):
        part_copy(k, sect).wait_send()

    @pl.loop(1, tiles)
    def _(k):
        table_copy(k, tile).wait_send()
        cell_copy(k, tile).wait_send()


def local(
    spectrum, courant, group_ratio, ocean_currents, elevation, sea_mask, owner_tile, ocean_slot
):
    bins, rows, columns = spectrum.shape
    tiles = lax.axis_size("tile")
    sects = lax.axis_size("sect")
    ocean_rows = elevation.shape[0] // columns
    angles = (np.arange(NDIR) + 0.5) * (2.0 * math.pi / NDIR)
    unit = CHUNKS * ABREAST * GROUP
    lines = -(-bins // unit) * unit
    extent = 2 * rows
    vmem = pl.BlockSpec(memory_space=pltpu.VMEM)
    hbm = pl.BlockSpec(memory_space=pltpu.HBM)
    dma = pltpu.SemaphoreType.DMA
    return pl.pallas_call(
        functools.partial(kernel, tiles, sects),
        out_shape=(
            jax.ShapeDtypeStruct(spectrum.shape, F32),
            jax.ShapeDtypeStruct((3, elevation.shape[0]), F32),
        ),
        in_specs=[hbm] * 9,
        out_specs=(hbm, vmem),
        scratch_shapes=[
            pltpu.SMEM((2 * NDIR + 8,), F32),
            pltpu.SMEM((NFREQ,), F32),
            pltpu.SMEM((NFREQ,), F32),
            pltpu.VMEM(ocean_currents.shape, F32),
            pltpu.VMEM((rows, columns), jnp.int32),
            pltpu.VMEM((rows, columns), jnp.int32),
            pltpu.VMEM((rows, columns), jnp.int32),
            pltpu.VMEM((3 * ocean_rows + 2 * rows, columns), F32),
            pltpu.VMEM((tiles, 3 * ocean_rows + 2 * rows, columns), F32),
            pltpu.VMEM((lines, rows, columns), F32),
            pltpu.VMEM((rows, lines, columns), F32),
            pltpu.VMEM((lines, rows, columns), F32),
            pltpu.VMEM((rows, lines, columns), F32),
            pltpu.VMEM((3, rows, 2 * columns), F32),
            pltpu.VMEM((4, extent, GROUP, columns), F32),
            pltpu.VMEM((5, lines, columns), F32),
            pltpu.VMEM((2, NFREQ, columns), F32),
            pltpu.VMEM((tiles, columns, rows * columns), BF16),
            pltpu.VMEM((3, rows, GROUP, columns), F32),
            pltpu.VMEM((sects, 3 * rows, columns), F32),
            pltpu.VMEM((tiles, 3 * rows, columns), F32),
            dma((8,)),
            dma,
            dma,
            dma((2, CHUNKS)),
            dma((2, CHUNKS)),
            dma((tiles,)),
            dma((tiles,)),
            dma((sects,)),
            dma((sects,)),
            dma((tiles,)),
            dma((tiles,)),
        ],
        compiler_params=pltpu.CompilerParams(
            collective_id=0, has_side_effects=True, vmem_limit_bytes=60 * 1024 * 1024
        ),
        cost_estimate=pl.CostEstimate(
            flops=bins * rows * columns * 200, bytes_accessed=8 * bins * rows * columns,
            transcendentals=0,
        ),
        name="coupling",
    )(
        jnp.asarray(np.concatenate([np.cos(angles), np.sin(angles), np.zeros(8)]), F32),
        courant,
        group_ratio,
        ocean_currents,
        elevation.reshape(ocean_rows, columns),
        sea_mask,
        owner_tile.reshape(rows, columns),
        ocean_slot.reshape(rows, columns),
        spectrum,
    )


def solution(mesh):
    in_specs = (
        P("sect", "tile", None),
        P(),
        P(),
        P(None, "tile"),
        P("tile"),
        P("tile", None),
        P("tile", None),
        P("tile"),
    )
    out_specs = (P("sect", "tile", None), P(None, "tile"))
    return jax.shard_map(local, mesh=mesh, in_specs=in_specs, out_specs=out_specs, check_vma=False)
```

```python
import functools
import math

import jax
import jax.numpy as jnp
import numpy as np
from jax import lax
from jax.experimental import pallas as pl
from jax.experimental.pallas import tpu as pltpu
from jax.sharding import PartitionSpec as P

NDIR = 36
NFREQ = 36
STEPS = 4
CHUNKS = 7
ABREAST = 3
GROUP = 8
COPIES = 6
MESH = pl.DeviceIdType.MESH
F32 = jnp.float32
BF16 = jnp.bfloat16


def split_bf16(x):
    high = x.astype(BF16)
    return high, (x - high.astype(F32)).astype(BF16)


def lanes_of(x):
    return jnp.concatenate([x[j : j + 1] for j in range(x.shape[0])], axis=1)


def kernel(
    tiles,
    sects,
    trig_hbm,
    courant_hbm,
    ratio_hbm,
    current_hbm,
    elevation_hbm,
    mask_hbm,
    owner_hbm,
    slot_hbm,
    spectrum_ref,
    out_ref,
    stress_ref,
    trig_ref,
    courant_ref,
    ratio_ref,
    current_ref,
    mask_ref,
    owner_ref,
    slot_ref,
    bundle,
    table,
    energy,
    packed,
    result,
    halo,
    flow,
    fields,
    scalars,
    by_freq,
    hots,
    sums,
    parts,
    cells,
    small_sem,
    load_sem,
    out_sem,
    halo_send,
    halo_recv,
    table_send,
    table_recv,
    part_send,
    part_recv,
    cell_send,
    cell_recv,
):
    tile = lax.axis_index("tile")
    sect = lax.axis_index("sect")
    bins = spectrum_ref.shape[0]
    rows, columns = mask_ref.shape
    half = rows // 2
    ocean_rows = elevation_hbm.shape[0]
    ocean_cells = ocean_rows * columns
    lines = halo.shape[1]
    per = lines // CHUNKS
    first = 3 * ocean_rows
    shift = columns.bit_length() - 1
    has_up = tile < tiles - 1
    has_down = tile > 0
    up = lax.rem(tile + 1, tiles)
    down = lax.rem(tile + tiles - 1, tiles)

    load = pltpu.make_async_copy(spectrum_ref, energy.at[pl.ds(0, bins)], load_sem)
    load.start()

    small = [
        (trig_hbm, trig_ref),
        (courant_hbm, courant_ref),
        (ratio_hbm, ratio_ref),
        (current_hbm, current_ref),
        (elevation_hbm, bundle.at[pl.ds(2 * ocean_rows, ocean_rows)]),
        (mask_hbm, mask_ref),
        (owner_hbm, owner_ref),
        (slot_hbm, slot_ref),
    ]
    small = [pltpu.make_async_copy(a, b, small_sem.at[i]) for i, (a, b) in enumerate(small)]
    for copy in small:
        copy.start()
    barrier = pltpu.get_barrier_semaphore()

    @pl.loop(1, tiles)
    def _(k):
        pl.semaphore_signal(
            barrier, inc=1, device_id=(sect, lax.rem(tile + k, tiles)), device_id_type=MESH
        )

    @pl.loop(1, sects)
    def _(k):
        pl.semaphore_signal(
            barrier, inc=1, device_id=(lax.rem(sect + k, sects), tile), device_id_type=MESH
        )

    spare = lines - bins
    energy_rows = energy.reshape(lines * rows, columns)
    result_rows = result.reshape(lines * rows, columns)
    for b in range(bins, lines):
        energy[b] = jnp.zeros((rows, columns), F32)

    def pack(g):
        for r in range(rows):
            packed[r, pl.ds(pl.multiple_of(g * GROUP, GROUP), GROUP), :] = energy_rows[
                pl.ds(g * GROUP * rows + r, GROUP, stride=rows), :
            ]

    def halo_copy(side, c):
        at = (pl.ds(side * half, half), pl.ds(pl.multiple_of(c * per, GROUP), per))
        return pltpu.make_async_remote_copy(
            src_ref=packed.at[at],
            dst_ref=halo.at[at],
            send_sem=halo_send.at[side, c],
            recv_sem=halo_recv.at[side, c],
            device_id=(sect, down if side == 0 else up),
            device_id_type=MESH,
        )

    for copy in small:
        copy.wait()
    for r in range(ocean_rows):
        at = pl.ds(r * columns, columns)
        bundle[pl.ds(r, 1), :] = current_ref[pl.ds(0, 1), at]
        bundle[pl.ds(ocean_rows + r, 1), :] = current_ref[pl.ds(1, 1), at]
    bundle[pl.ds(first, rows), :] = (owner_ref[...] * ocean_cells + slot_ref[...]).astype(F32)
    bundle[pl.ds(first + rows, rows), :] = mask_ref[...].astype(F32)
    table[tile] = bundle[...]
    pl.semaphore_wait(barrier, tiles + sects - 2)

    def table_copy(k, slot):
        return pltpu.make_async_remote_copy(
            src_ref=bundle,
            dst_ref=table.at[slot],
            send_sem=table_send.at[k],
            recv_sem=table_recv.at[slot],
            device_id=(sect, lax.rem(tile + k, tiles)),
            device_id_type=MESH,
        )

    @pl.loop(1, tiles)
    def _(k):
        table_copy(k, tile).start()

    load.wait()

    @pl.loop(0, CHUNKS)
    def _(c):
        for g in range(per // GROUP):
            pack(c * (per // GROUP) + g)

        @pl.when(has_down)
        def _():
            halo_copy(0, c).start()

        @pl.when(has_up)
        def _():
            halo_copy(1, c).start()

    @pl.when(jnp.logical_not(has_up))
    def _():
        halo[pl.ds(0, half)] = jnp.zeros((half, lines, columns), F32)

    @pl.when(jnp.logical_not(has_down))
    def _():
        halo[pl.ds(half, half)] = jnp.zeros((half, lines, columns), F32)

    start = sect * bins
    first_dir, first_freq = start // NFREQ, start % NFREQ
    for i in range(NFREQ):
        f = first_freq + i
        f = jnp.where(f >= NFREQ, f - NFREQ, f)
        by_freq[0, pl.ds(i, 1), :] = jnp.full((1, columns), courant_ref[f], F32)
        by_freq[1, pl.ds(i, 1), :] = jnp.full((1, columns), ratio_ref[f], F32)
    speed, ratio = by_freq[0], by_freq[1]
    wrapped = lax.broadcasted_iota(jnp.int32, (NFREQ, columns), 0) + first_freq >= NFREQ
    scale = 4.0 / (NDIR * NFREQ)
    for begin in range(0, bins, NFREQ):
        count = min(NFREQ, bins - begin)
        d = first_dir + begin // NFREQ
        c = jnp.where(wrapped, trig_ref[d + 1], trig_ref[d])
        s = jnp.where(wrapped, trig_ref[NDIR + d + 1], trig_ref[NDIR + d])
        values = (
            speed * c,
            speed * s,
            (ratio * (1.0 + c * c) - 0.5) * scale,
            (ratio * c * s) * scale,
            (ratio * (1.0 + s * s) - 0.5) * scale,
        )
        for q in range(5):
            scalars[q, pl.ds(begin, count), :] = values[q][:count]
    if spare:
        for q in range(5):
            scalars[q, pl.ds(bins, spare), :] = jnp.zeros((spare, columns), F32)
    sums[...] = jnp.zeros_like(sums)

    @pl.loop(1, tiles)
    def _(k):
        table_copy(k, lax.rem(tile + tiles - k, tiles)).wait_recv()

    sub = lax.broadcasted_iota(jnp.int32, (rows, columns), 0)
    upper = sub < half
    valid = (upper & has_up) | (jnp.logical_not(upper) & has_down)

    def ring(start):
        own = table[tile, pl.ds(start, rows), :]
        other = jnp.where(
            upper, table[up, pl.ds(start, rows), :], table[down, pl.ds(start, rows), :]
        )
        return own, other

    target_own, target_halo = ring(first)
    mask_own, mask_halo = ring(first + rows)
    mask_halo = jnp.where(valid, mask_halo, 0.0)
    target_own = target_own.astype(jnp.int32)
    target_halo = target_halo.astype(jnp.int32)

    table_rows = tiles * ocean_rows
    pieces = []
    for field in range(3):
        whole = table[:, pl.ds(field * ocean_rows, ocean_rows), :].reshape(table_rows, columns)
        high, low = split_bf16(whole.T)
        pieces.append(jnp.concatenate([high, low], axis=1))
    lookup = jnp.concatenate(pieces, axis=0)
    row_ids = lax.broadcasted_iota(jnp.int32, (table_rows, 2 * columns), 0)
    lane_ids = lax.broadcasted_iota(jnp.int32, (columns, 2 * columns), 0)
    for j in range(rows):
        index = jnp.concatenate([target_own[j : j + 1], target_halo[j : j + 1]], axis=1)
        hot = jnp.where(row_ids == index >> shift, 1.0, 0.0).astype(BF16)
        found = jnp.dot(
            lookup, jnp.concatenate([hot, hot], axis=0), preferred_element_type=F32
        )
        chosen = lane_ids == (index & (columns - 1))
        for field in range(3):
            value = jnp.sum(
                jnp.where(chosen, found[field * columns : (field + 1) * columns], 0.0),
                axis=0,
                keepdims=True,
            )
            flow[field, pl.ds(j, 1), :] = value

    def east(x):
        return pltpu.roll(x, columns - 1, 1)

    def west(x):
        return pltpu.roll(x, 1, 1)

    u_own = flow[0, :, pl.ds(0, columns)]
    u_halo = jnp.where(valid, flow[0, :, pl.ds(columns, columns)], 0.0)
    v_own = flow[1, :, pl.ds(0, columns)]
    v_halo = jnp.where(valid, flow[1, :, pl.ds(columns, columns)], 0.0)
    factor = (1.0 + flow[2, :, pl.ds(0, columns)]) * mask_own
    extent = rows + 2 * half

    def in_order(own, other):
        return jnp.concatenate([other[half:], own, other[:half]], axis=0)

    u_all = in_order(u_own, u_halo)
    v_all = in_order(v_own, v_halo)
    m_all = in_order(mask_own, mask_halo)
    ux_all = 0.5 * (u_all + east(u_all))
    uw_all = west(ux_all)
    vy_all = 0.5 * (v_all[:-1] + v_all[1:])
    for j in range(extent):
        fields[0, j] = jnp.broadcast_to(ux_all[j : j + 1], (GROUP, columns))
        fields[1, j] = jnp.broadcast_to(uw_all[j : j + 1], (GROUP, columns))
        fields[2, j] = jnp.broadcast_to(m_all[j : j + 1], (GROUP, columns))
        if j < extent - 1:
            fields[3, j] = jnp.broadcast_to(vy_all[j : j + 1], (GROUP, columns))

    class Group:
        def __init__(self, begin):
            begin = pl.multiple_of(begin, GROUP)
            self.begin = begin
            self.yp, self.ym, self.xm, self.xpw, self.c0 = {}, {}, {}, {}, {}
            self.sx = scalars[0, pl.ds(begin, GROUP), :]
            self.sy = scalars[1, pl.ds(begin, GROUP), :]
            e = {}
            for j in range(rows):
                e[half + j] = packed[j, pl.ds(begin, GROUP), :]
                e[half + rows + j if j < half else j - half] = halo[j, pl.ds(begin, GROUP), :]
            self.levels = [e] + [{} for _ in range(STEPS)]

        def coefficients(self, j):
            ay = self.sy + fields[3, j]
            self.yp[j], self.ym[j] = jnp.maximum(ay, 0.0), jnp.minimum(ay, 0.0)
            if j:
                ax = self.sx + fields[0, j]
                aw = self.sx + fields[1, j]
                self.xm[j] = jnp.minimum(ax, 0.0)
                self.xpw[j] = jnp.maximum(aw, 0.0)
                out_x = jnp.maximum(ax, 0.0) - jnp.minimum(aw, 0.0)
                self.c0[j] = (1.0 - out_x) - (self.yp[j] - self.ym[j - 1])

        def advance(self, step, j):
            old = self.levels[step - 1]
            value = self.c0[j] * old[j] - self.xm[j] * east(old[j]) + self.xpw[j] * west(old[j])
            value = value - self.ym[j] * old[j + 1] + self.yp[j - 1] * old[j - 1]
            self.levels[step][j] = fields[2, j] * value

    def abreast(begin):
        members = [Group(begin + i * GROUP) for i in range(ABREAST)]
        for member in members:
            member.coefficients(0)
        for wave in range(1, extent + 2 * STEPS):
            for member in members:
                if wave < extent - 1:
                    member.coefficients(wave)
            for step in range(STEPS, 0, -1):
                j = wave - 2 * (step - 1)
                if step <= j < extent - step:
                    for member in members:
                        member.advance(step, j)
        for member in members:
            for j in range(rows):
                result_rows[pl.ds(member.begin * rows + j, GROUP, stride=rows), :] = (
                    member.levels[STEPS][half + j]
                )
        for k in range(3):
            weights = [scalars[2 + k, pl.ds(member.begin, GROUP), :] for member in members]
            for j in range(rows):
                added = sums[k, j]
                for member, weight in zip(members, weights):
                    added = added + weight * member.levels[STEPS][half + j]
                sums[k, j] = added

    cell_count = rows * columns
    ocean_ids = lax.broadcasted_iota(jnp.int32, (ocean_rows, cell_count), 0) + tile * ocean_rows

    def index_of(source):
        return lanes_of(table[source, pl.ds(first, rows), :].astype(jnp.int32))

    def row_hot_of(source):
        return ocean_ids == index_of(source) >> shift

    @pl.loop(0, tiles)
    def _(source):
        lane = index_of(source) & (columns - 1)
        ids = lax.broadcasted_iota(jnp.int32, (columns, cell_count), 0)
        hots[source] = jnp.where(ids == lane, 1.0, 0.0).astype(BF16)

    def product(left, source):
        return lax.dot_general(
            left, hots[source], (((1,), (1,)), ((), ())), preferred_element_type=F32
        )

    def count_tile(source, counts):
        return counts + product(jnp.where(row_hot_of(source), 1.0, 0.0).astype(BF16), source)

    counts = lax.fori_loop(0, tiles, count_tile, jnp.zeros((ocean_rows, columns), F32))
    counts = jnp.maximum(counts, 1.0)

    @pl.loop(0, CHUNKS)
    def _(c):
        @pl.when(has_up)
        def _():
            halo_copy(0, c).wait_recv()

        @pl.when(has_down)
        def _():
            halo_copy(1, c).wait_recv()

        @pl.loop(0, per // (GROUP * ABREAST))
        def _(i):
            abreast(c * per + i * (GROUP * ABREAST))

    store = pltpu.make_async_copy(result.at[pl.ds(0, bins)], out_ref, out_sem)
    store.start()

    def part_copy(k, slot):
        return pltpu.make_async_remote_copy(
            src_ref=parts.at[sect],
            dst_ref=parts.at[slot],
            send_sem=part_send.at[k],
            recv_sem=part_recv.at[slot],
            device_id=(lax.rem(sect + k, sects), tile),
            device_id_type=MESH,
        )

    for k in range(3):
        for j in range(rows):
            parts[sect, pl.ds(k * rows + j, 1), :] = jnp.sum(sums[k, j], axis=0, keepdims=True)
    for k in range(1, sects):
        part_copy(k, sect).start()

    for k in range(1, sects):
        part_copy(k, lax.rem(sect + sects - k, sects)).wait_recv()
    total = parts[0]
    for k in range(1, sects):
        total = total + parts[k]
    cells[tile] = total * jnp.concatenate([factor] * 3, axis=0)

    def cell_copy(k, slot):
        return pltpu.make_async_remote_copy(
            src_ref=cells.at[tile],
            dst_ref=cells.at[slot],
            send_sem=cell_send.at[k],
            recv_sem=cell_recv.at[slot],
            device_id=(sect, lax.rem(tile + k, tiles)),
            device_id_type=MESH,
        )

    @pl.loop(1, tiles)
    def _(k):
        cell_copy(k, tile).start()

    def add_tile(source, acc):
        stress = cells[source]
        row_hot = row_hot_of(source)
        highs, lows = [], []
        for k in range(3):
            high, low = split_bf16(stress[k * rows : (k + 1) * rows])
            for value, into in ((high, highs), (low, lows)):
                value = lanes_of(value.astype(F32))
                into.append(jnp.where(row_hot, value, 0.0).astype(BF16))
        return acc + product(jnp.concatenate(highs + lows, axis=0), source)

    acc = add_tile(tile, jnp.zeros((6 * ocean_rows, columns), F32))

    def add_other(k, acc):
        source = lax.rem(tile + tiles - k, tiles)
        cell_copy(k, source).wait_recv()
        return add_tile(source, acc)

    acc = lax.fori_loop(1, tiles, add_other, acc)
    for k in range(3):
        high = acc[k * ocean_rows : (k + 1) * ocean_rows]
        low = acc[(3 + k) * ocean_rows : (4 + k) * ocean_rows]
        mean = (high + low) / counts
        for r in range(ocean_rows):
            stress_ref[pl.ds(k, 1), pl.ds(r * columns, columns)] = mean[r : r + 1]

    store.wait()
    for c in range(CHUNKS):

        @pl.when(has_down)
        def _():
            halo_copy(0, c).wait_send()

        @pl.when(has_up)
        def _():
            halo_copy(1, c).wait_send()

    for k in range(1, sects):
        part_copy(k, sect).wait_send()

    @pl.loop(1, tiles)
    def _(k):
        table_copy(k, tile).wait_send()
        cell_copy(k, tile).wait_send()


def hand_on(spectrum_ref, stress_ref, spectrum_out, stress_out, sems):
    bins = spectrum_ref.shape[0]
    copies = [pltpu.make_async_copy(stress_ref, stress_out, sems.at[COPIES])]
    for i in range(COPIES):
        at = pl.ds(bins * i // COPIES, bins * (i + 1) // COPIES - bins * i // COPIES)
        copies.append(
            pltpu.make_async_copy(spectrum_ref.at[at], spectrum_out.at[at], sems.at[i])
        )
    for copy in copies:
        copy.start()
    for copy in copies:
        copy.wait()


def local(
    spectrum, courant, group_ratio, ocean_currents, elevation, sea_mask, owner_tile, ocean_slot
):
    bins, rows, columns = spectrum.shape
    tiles = lax.axis_size("tile")
    sects = lax.axis_size("sect")
    ocean_rows = elevation.shape[0] // columns
    angles = (np.arange(NDIR) + 0.5) * (2.0 * math.pi / NDIR)
    unit = CHUNKS * ABREAST * GROUP
    lines = -(-bins // unit) * unit
    extent = 2 * rows
    vmem = pl.BlockSpec(memory_space=pltpu.VMEM)
    hbm = pl.BlockSpec(memory_space=pltpu.HBM)
    dma = pltpu.SemaphoreType.DMA
    new_spectrum, stress = pl.pallas_call(
        functools.partial(kernel, tiles, sects),
        out_shape=(
            jax.ShapeDtypeStruct(spectrum.shape, F32),
            jax.ShapeDtypeStruct((3, elevation.shape[0]), F32),
        ),
        in_specs=[hbm] * 9,
        out_specs=(hbm, vmem),
        scratch_shapes=[
            pltpu.SMEM((2 * NDIR + 8,), F32),
            pltpu.SMEM((NFREQ,), F32),
            pltpu.SMEM((NFREQ,), F32),
            pltpu.VMEM(ocean_currents.shape, F32),
            pltpu.VMEM((rows, columns), jnp.int32),
            pltpu.VMEM((rows, columns), jnp.int32),
            pltpu.VMEM((rows, columns), jnp.int32),
            pltpu.VMEM((3 * ocean_rows + 2 * rows, columns), F32),
            pltpu.VMEM((tiles, 3 * ocean_rows + 2 * rows, columns), F32),
            pltpu.VMEM((lines, rows, columns), F32),
            pltpu.VMEM((rows, lines, columns), F32),
            pltpu.VMEM((lines, rows, columns), F32),
            pltpu.VMEM((rows, lines, columns), F32),
            pltpu.VMEM((3, rows, 2 * columns), F32),
            pltpu.VMEM((4, extent, GROUP, columns), F32),
            pltpu.VMEM((5, lines, columns), F32),
            pltpu.VMEM((2, NFREQ, columns), F32),
            pltpu.VMEM((tiles, columns, rows * columns), BF16),
            pltpu.VMEM((3, rows, GROUP, columns), F32),
            pltpu.VMEM((sects, 3 * rows, columns), F32),
            pltpu.VMEM((tiles, 3 * rows, columns), F32),
            dma((8,)),
            dma,
            dma,
            dma((2, CHUNKS)),
            dma((2, CHUNKS)),
            dma((tiles,)),
            dma((tiles,)),
            dma((sects,)),
            dma((sects,)),
            dma((tiles,)),
            dma((tiles,)),
        ],
        compiler_params=pltpu.CompilerParams(
            collective_id=0, has_side_effects=True, vmem_limit_bytes=60 * 1024 * 1024
        ),
        cost_estimate=pl.CostEstimate(
            flops=bins * rows * columns * 200, bytes_accessed=8 * bins * rows * columns,
            transcendentals=0,
        ),
        name="coupling",
    )(
        jnp.asarray(np.concatenate([np.cos(angles), np.sin(angles), np.zeros(8)]), F32),
        courant,
        group_ratio,
        ocean_currents,
        elevation.reshape(ocean_rows, columns),
        sea_mask,
        owner_tile.reshape(rows, columns),
        ocean_slot.reshape(rows, columns),
        spectrum,
    )
    return pl.pallas_call(
        hand_on,
        out_shape=(
            jax.ShapeDtypeStruct(new_spectrum.shape, F32),
            jax.ShapeDtypeStruct(stress.shape, F32),
        ),
        in_specs=[hbm, hbm],
        out_specs=(hbm, hbm),
        scratch_shapes=[dma((COPIES + 1,))],
        compiler_params=pltpu.CompilerParams(vmem_limit_bytes=60 * 1024 * 1024),
        name="hand_on",
    )(new_spectrum, stress)


def solution(mesh):
    in_specs = (
        P("sect", "tile", None),
        P(),
        P(),
        P(None, "tile"),
        P("tile"),
        P("tile", None),
        P("tile", None),
        P("tile"),
    )
    out_specs = (P("sect", "tile", None), P(None, "tile"))
    return jax.shard_map(local, mesh=mesh, in_specs=in_specs, out_specs=out_specs, check_vma=False)
```

```python
import functools
import math

import jax
import jax.numpy as jnp
import numpy as np
from jax import lax
from jax.experimental import pallas as pl
from jax.experimental.pallas import tpu as pltpu
from jax.sharding import PartitionSpec as P

NDIR = 36
NFREQ = 36
STEPS = 4
CHUNKS = 7
ABREAST = 3
GROUP = 8
COPIES = 6
MESH = pl.DeviceIdType.MESH
F32 = jnp.float32
BF16 = jnp.bfloat16


def split_bf16(x):
    high = x.astype(BF16)
    return high, (x - high.astype(F32)).astype(BF16)


def lanes_of(x):
    return jnp.concatenate([x[j : j + 1] for j in range(x.shape[0])], axis=1)


def kernel(
    tiles,
    sects,
    trig_hbm,
    courant_hbm,
    ratio_hbm,
    current_hbm,
    elevation_hbm,
    mask_hbm,
    owner_hbm,
    slot_hbm,
    spectrum_ref,
    out_ref,
    stress_ref,
    trig_ref,
    courant_ref,
    ratio_ref,
    current_ref,
    mask_ref,
    owner_ref,
    slot_ref,
    bundle,
    table,
    energy,
    packed,
    result,
    halo,
    flow,
    fields,
    scalars,
    by_freq,
    hots,
    sums,
    parts,
    cells,
    small_sem,
    load_sem,
    out_sem,
    halo_send,
    halo_recv,
    table_send,
    table_recv,
    part_send,
    part_recv,
    cell_send,
    cell_recv,
):
    tile = lax.axis_index("tile")
    sect = lax.axis_index("sect")
    bins = spectrum_ref.shape[0]
    rows, columns = mask_ref.shape
    half = rows // 2
    ocean_rows = elevation_hbm.shape[0]
    ocean_cells = ocean_rows * columns
    lines = halo.shape[1]
    per = lines // CHUNKS
    first = 3 * ocean_rows
    shift = columns.bit_length() - 1
    has_up = tile < tiles - 1
    has_down = tile > 0
    up = lax.rem(tile + 1, tiles)
    down = lax.rem(tile + tiles - 1, tiles)

    load = pltpu.make_async_copy(spectrum_ref, energy.at[pl.ds(0, bins)], load_sem)
    load.start()

    small = [
        (trig_hbm, trig_ref),
        (courant_hbm, courant_ref),
        (ratio_hbm, ratio_ref),
        (current_hbm, current_ref),
        (elevation_hbm, bundle.at[pl.ds(2 * ocean_rows, ocean_rows)]),
        (mask_hbm, mask_ref),
        (owner_hbm, owner_ref),
        (slot_hbm, slot_ref),
    ]
    small = [pltpu.make_async_copy(a, b, small_sem.at[i]) for i, (a, b) in enumerate(small)]
    for copy in small:
        copy.start()
    barrier = pltpu.get_barrier_semaphore()

    @pl.loop(1, tiles)
    def _(k):
        pl.semaphore_signal(
            barrier, inc=1, device_id=(sect, lax.rem(tile + k, tiles)), device_id_type=MESH
        )

    @pl.loop(1, sects)
    def _(k):
        pl.semaphore_signal(
            barrier, inc=1, device_id=(lax.rem(sect + k, sects), tile), device_id_type=MESH
        )

    spare = lines - bins
    energy_rows = energy.reshape(lines * rows, columns)
    result_rows = result.reshape(lines * rows, columns)
    for b in range(bins, lines):
        energy[b] = jnp.zeros((rows, columns), F32)

    def pack(g):
        for r in range(rows):
            packed[r, pl.ds(pl.multiple_of(g * GROUP, GROUP), GROUP), :] = energy_rows[
                pl.ds(g * GROUP * rows + r, GROUP, stride=rows), :
            ]

    def halo_copy(side, c):
        at = (pl.ds(side * half, half), pl.ds(pl.multiple_of(c * per, GROUP), per))
        return pltpu.make_async_remote_copy(
            src_ref=packed.at[at],
            dst_ref=halo.at[at],
            send_sem=halo_send.at[side, c],
            recv_sem=halo_recv.at[side, c],
            device_id=(sect, down if side == 0 else up),
            device_id_type=MESH,
        )

    for copy in small:
        copy.wait()
    for r in range(ocean_rows):
        at = pl.ds(r * columns, columns)
        bundle[pl.ds(r, 1), :] = current_ref[pl.ds(0, 1), at]
        bundle[pl.ds(ocean_rows + r, 1), :] = current_ref[pl.ds(1, 1), at]
    bundle[pl.ds(first, rows), :] = (owner_ref[...] * ocean_cells + slot_ref[...]).astype(F32)
    bundle[pl.ds(first + rows, rows), :] = mask_ref[...].astype(F32)
    table[tile] = bundle[...]
    pl.semaphore_wait(barrier, tiles + sects - 2)

    def table_copy(k, slot):
        return pltpu.make_async_remote_copy(
            src_ref=bundle,
            dst_ref=table.at[slot],
            send_sem=table_send.at[k],
            recv_sem=table_recv.at[slot],
            device_id=(sect, lax.rem(tile + k, tiles)),
            device_id_type=MESH,
        )

    @pl.loop(1, tiles)
    def _(k):
        table_copy(k, tile).start()

    load.wait()

    @pl.loop(0, CHUNKS)
    def _(c):
        for g in range(per // GROUP):
            pack(c * (per // GROUP) + g)

        @pl.when(has_down)
        def _():
            halo_copy(0, c).start()

        @pl.when(has_up)
        def _():
            halo_copy(1, c).start()

    @pl.when(jnp.logical_not(has_up))
    def _():
        halo[pl.ds(0, half)] = jnp.zeros((half, lines, columns), F32)

    @pl.when(jnp.logical_not(has_down))
    def _():
        halo[pl.ds(half, half)] = jnp.zeros((half, lines, columns), F32)

    start = sect * bins
    first_dir, first_freq = start // NFREQ, start % NFREQ
    for i in range(NFREQ):
        f = first_freq + i
        f = jnp.where(f >= NFREQ, f - NFREQ, f)
        by_freq[0, pl.ds(i, 1), :] = jnp.full((1, columns), courant_ref[f], F32)
        by_freq[1, pl.ds(i, 1), :] = jnp.full((1, columns), ratio_ref[f], F32)
    speed, ratio = by_freq[0], by_freq[1]
    wrapped = lax.broadcasted_iota(jnp.int32, (NFREQ, columns), 0) + first_freq >= NFREQ
    scale = 4.0 / (NDIR * NFREQ)
    for begin in range(0, bins, NFREQ):
        count = min(NFREQ, bins - begin)
        d = first_dir + begin // NFREQ
        c = jnp.where(wrapped, trig_ref[d + 1], trig_ref[d])
        s = jnp.where(wrapped, trig_ref[NDIR + d + 1], trig_ref[NDIR + d])
        values = (
            speed * c,
            speed * s,
            (ratio * (1.0 + c * c) - 0.5) * scale,
            (ratio * c * s) * scale,
            (ratio * (1.0 + s * s) - 0.5) * scale,
        )
        for q in range(5):
            scalars[q, pl.ds(begin, count), :] = values[q][:count]
    if spare:
        for q in range(5):
            scalars[q, pl.ds(bins, spare), :] = jnp.zeros((spare, columns), F32)
    sums[...] = jnp.zeros_like(sums)

    @pl.loop(1, tiles)
    def _(k):
        table_copy(k, lax.rem(tile + tiles - k, tiles)).wait_recv()

    sub = lax.broadcasted_iota(jnp.int32, (rows, columns), 0)
    upper = sub < half
    valid = (upper & has_up) | (jnp.logical_not(upper) & has_down)

    def ring(start):
        own = table[tile, pl.ds(start, rows), :]
        other = jnp.where(
            upper, table[up, pl.ds(start, rows), :], table[down, pl.ds(start, rows), :]
        )
        return own, other

    target_own, target_halo = ring(first)
    mask_own, mask_halo = ring(first + rows)
    mask_halo = jnp.where(valid, mask_halo, 0.0)
    target_own = target_own.astype(jnp.int32)
    target_halo = target_halo.astype(jnp.int32)

    table_rows = tiles * ocean_rows
    pieces = []
    for field in range(3):
        whole = table[:, pl.ds(field * ocean_rows, ocean_rows), :].reshape(table_rows, columns)
        high, low = split_bf16(whole.T)
        pieces.append(jnp.concatenate([high, low], axis=1))
    lookup = jnp.concatenate(pieces, axis=0)
    row_ids = lax.broadcasted_iota(jnp.int32, (table_rows, 2 * columns), 0)
    lane_ids = lax.broadcasted_iota(jnp.int32, (columns, 2 * columns), 0)
    for j in range(rows):
        index = jnp.concatenate([target_own[j : j + 1], target_halo[j : j + 1]], axis=1)
        hot = jnp.where(row_ids == index >> shift, 1.0, 0.0).astype(BF16)
        found = jnp.dot(
            lookup, jnp.concatenate([hot, hot], axis=0), preferred_element_type=F32
        )
        chosen = lane_ids == (index & (columns - 1))
        for field in range(3):
            value = jnp.sum(
                jnp.where(chosen, found[field * columns : (field + 1) * columns], 0.0),
                axis=0,
                keepdims=True,
            )
            flow[field, pl.ds(j, 1), :] = value

    def east(x):
        return pltpu.roll(x, columns - 1, 1)

    def west(x):
        return pltpu.roll(x, 1, 1)

    u_own = flow[0, :, pl.ds(0, columns)]
    u_halo = jnp.where(valid, flow[0, :, pl.ds(columns, columns)], 0.0)
    v_own = flow[1, :, pl.ds(0, columns)]
    v_halo = jnp.where(valid, flow[1, :, pl.ds(columns, columns)], 0.0)
    factor = (1.0 + flow[2, :, pl.ds(0, columns)]) * mask_own
    extent = rows + 2 * half

    def in_order(own, other):
        return jnp.concatenate([other[half:], own, other[:half]], axis=0)

    u_all = in_order(u_own, u_halo)
    v_all = in_order(v_own, v_halo)
    m_all = in_order(mask_own, mask_halo)
    ux_all = 0.5 * (u_all + east(u_all))
    uw_all = west(ux_all)
    vy_all = 0.5 * (v_all[:-1] + v_all[1:])
    for j in range(extent):
        fields[0, j] = jnp.broadcast_to(ux_all[j : j + 1], (GROUP, columns))
        fields[1, j] = jnp.broadcast_to(uw_all[j : j + 1], (GROUP, columns))
        fields[2, j] = jnp.broadcast_to(m_all[j : j + 1], (GROUP, columns))
        if j < extent - 1:
            fields[3, j] = jnp.broadcast_to(vy_all[j : j + 1], (GROUP, columns))

    class Group:
        def __init__(self, begin):
            begin = pl.multiple_of(begin, GROUP)
            self.begin = begin
            self.yp, self.ym, self.xm, self.xpw, self.c0 = {}, {}, {}, {}, {}
            self.sx = scalars[0, pl.ds(begin, GROUP), :]
            self.sy = scalars[1, pl.ds(begin, GROUP), :]
            e = {}
            for j in range(rows):
                e[half + j] = packed[j, pl.ds(begin, GROUP), :]
                e[half + rows + j if j < half else j - half] = halo[j, pl.ds(begin, GROUP), :]
            self.levels = [e] + [{} for _ in range(STEPS)]

        def coefficients(self, j):
            ay = self.sy + fields[3, j]
            self.yp[j], self.ym[j] = jnp.maximum(ay, 0.0), jnp.minimum(ay, 0.0)
            if j:
                ax = self.sx + fields[0, j]
                aw = self.sx + fields[1, j]
                self.xm[j] = jnp.minimum(ax, 0.0)
                self.xpw[j] = jnp.maximum(aw, 0.0)
                out_x = jnp.maximum(ax, 0.0) - jnp.minimum(aw, 0.0)
                self.c0[j] = (1.0 - out_x) - (self.yp[j] - self.ym[j - 1])

        def advance(self, step, j):
            old = self.levels[step - 1]
            value = self.c0[j] * old[j] - self.xm[j] * east(old[j]) + self.xpw[j] * west(old[j])
            value = value - self.ym[j] * old[j + 1] + self.yp[j - 1] * old[j - 1]
            self.levels[step][j] = fields[2, j] * value

    def abreast(begin):
        members = [Group(begin + i * GROUP) for i in range(ABREAST)]
        for member in members:
            member.coefficients(0)
        for wave in range(1, extent + 2 * STEPS):
            for member in members:
                if wave < extent - 1:
                    member.coefficients(wave)
            for step in range(STEPS, 0, -1):
                j = wave - 2 * (step - 1)
                if step <= j < extent - step:
                    for member in members:
                        member.advance(step, j)
        for member in members:
            for j in range(rows):
                result_rows[pl.ds(member.begin * rows + j, GROUP, stride=rows), :] = (
                    member.levels[STEPS][half + j]
                )
        for k in range(3):
            weights = [scalars[2 + k, pl.ds(member.begin, GROUP), :] for member in members]
            for j in range(rows):
                added = sums[k, j]
                for member, weight in zip(members, weights):
                    added = added + weight * member.levels[STEPS][half + j]
                sums[k, j] = added

    cell_count = rows * columns
    ocean_ids = lax.broadcasted_iota(jnp.int32, (ocean_rows, cell_count), 0) + tile * ocean_rows

    def index_of(source):
        return lanes_of(table[source, pl.ds(first, rows), :].astype(jnp.int32))

    def row_hot_of(source):
        return ocean_ids == index_of(source) >> shift

    @pl.loop(0, tiles)
    def _(source):
        lane = index_of(source) & (columns - 1)
        ids = lax.broadcasted_iota(jnp.int32, (columns, cell_count), 0)
        hots[source] = jnp.where(ids == lane, 1.0, 0.0).astype(BF16)

    def product(left, source):
        return lax.dot_general(
            left, hots[source], (((1,), (1,)), ((), ())), preferred_element_type=F32
        )

    def count_tile(source, counts):
        return counts + product(jnp.where(row_hot_of(source), 1.0, 0.0).astype(BF16), source)

    counts = lax.fori_loop(0, tiles, count_tile, jnp.zeros((ocean_rows, columns), F32))
    counts = jnp.maximum(counts, 1.0)

    @pl.loop(0, CHUNKS)
    def _(c):
        @pl.when(has_up)
        def _():
            halo_copy(0, c).wait_recv()

        @pl.when(has_down)
        def _():
            halo_copy(1, c).wait_recv()

        @pl.loop(0, per // (GROUP * ABREAST))
        def _(i):
            abreast(c * per + i * (GROUP * ABREAST))

    store = pltpu.make_async_copy(result.at[pl.ds(0, bins)], out_ref, out_sem)
    store.start()

    def part_copy(k, slot):
        return pltpu.make_async_remote_copy(
            src_ref=parts.at[sect],
            dst_ref=parts.at[slot],
            send_sem=part_send.at[k],
            recv_sem=part_recv.at[slot],
            device_id=(lax.rem(sect + k, sects), tile),
            device_id_type=MESH,
        )

    for k in range(3):
        for j in range(rows):
            parts[sect, pl.ds(k * rows + j, 1), :] = jnp.sum(sums[k, j], axis=0, keepdims=True)
    for k in range(1, sects):
        part_copy(k, sect).start()

    for k in range(1, sects):
        part_copy(k, lax.rem(sect + sects - k, sects)).wait_recv()
    total = parts[0]
    for k in range(1, sects):
        total = total + parts[k]
    cells[tile] = total * jnp.concatenate([factor] * 3, axis=0)

    def cell_copy(k, slot):
        return pltpu.make_async_remote_copy(
            src_ref=cells.at[tile],
            dst_ref=cells.at[slot],
            send_sem=cell_send.at[k],
            recv_sem=cell_recv.at[slot],
            device_id=(sect, lax.rem(tile + k, tiles)),
            device_id_type=MESH,
        )

    @pl.loop(1, tiles)
    def _(k):
        cell_copy(k, tile).start()

    def add_tile(source, acc):
        stress = cells[source]
        row_hot = row_hot_of(source)
        highs, lows = [], []
        for k in range(3):
            high, low = split_bf16(stress[k * rows : (k + 1) * rows])
            for value, into in ((high, highs), (low, lows)):
                value = lanes_of(value.astype(F32))
                into.append(jnp.where(row_hot, value, 0.0).astype(BF16))
        return acc + product(jnp.concatenate(highs + lows, axis=0), source)

    acc = add_tile(tile, jnp.zeros((6 * ocean_rows, columns), F32))

    def add_other(k, acc):
        source = lax.rem(tile + tiles - k, tiles)
        cell_copy(k, source).wait_recv()
        return add_tile(source, acc)

    acc = lax.fori_loop(1, tiles, add_other, acc)
    for k in range(3):
        high = acc[k * ocean_rows : (k + 1) * ocean_rows]
        low = acc[(3 + k) * ocean_rows : (4 + k) * ocean_rows]
        mean = (high + low) / counts
        for r in range(ocean_rows):
            stress_ref[pl.ds(k, 1), pl.ds(r * columns, columns)] = mean[r : r + 1]

    store.wait()
    for c in range(CHUNKS):

        @pl.when(has_down)
        def _():
            halo_copy(0, c).wait_send()

        @pl.when(has_up)
        def _():
            halo_copy(1, c).wait_send()

    for k in range(1, sects):
        part_copy(k, sect).wait_send()

    @pl.loop(1, tiles)
    def _(k):
        table_copy(k, tile).wait_send()
        cell_copy(k, tile).wait_send()


def hand_on(spectrum_ref, stress_ref, spectrum_out, stress_out, held, held_stress, into, out_of):
    bins = spectrum_ref.shape[0]
    loads = [pltpu.make_async_copy(stress_ref, held_stress, into.at[COPIES])]
    stores = [pltpu.make_async_copy(held_stress, stress_out, out_of.at[COPIES])]
    for i in range(COPIES):
        begin, end = bins * i // COPIES, bins * (i + 1) // COPIES
        at = pl.ds(begin, end - begin)
        loads.append(pltpu.make_async_copy(spectrum_ref.at[at], held.at[at], into.at[i]))
        stores.append(pltpu.make_async_copy(held.at[at], spectrum_out.at[at], out_of.at[i]))
    for load in loads:
        load.start()
    for load, store in zip(loads, stores):
        load.wait()
        store.start()
    for store in stores:
        store.wait()


def local(
    spectrum, courant, group_ratio, ocean_currents, elevation, sea_mask, owner_tile, ocean_slot
):
    bins, rows, columns = spectrum.shape
    tiles = lax.axis_size("tile")
    sects = lax.axis_size("sect")
    ocean_rows = elevation.shape[0] // columns
    angles = (np.arange(NDIR) + 0.5) * (2.0 * math.pi / NDIR)
    unit = CHUNKS * ABREAST * GROUP
    lines = -(-bins // unit) * unit
    extent = 2 * rows
    vmem = pl.BlockSpec(memory_space=pltpu.VMEM)
    hbm = pl.BlockSpec(memory_space=pltpu.HBM)
    dma = pltpu.SemaphoreType.DMA
    new_spectrum, stress = pl.pallas_call(
        functools.partial(kernel, tiles, sects),
        out_shape=(
            jax.ShapeDtypeStruct(spectrum.shape, F32),
            jax.ShapeDtypeStruct((3, elevation.shape[0]), F32),
        ),
        in_specs=[hbm] * 9,
        out_specs=(hbm, vmem),
        scratch_shapes=[
            pltpu.SMEM((2 * NDIR + 8,), F32),
            pltpu.SMEM((NFREQ,), F32),
            pltpu.SMEM((NFREQ,), F32),
            pltpu.VMEM(ocean_currents.shape, F32),
            pltpu.VMEM((rows, columns), jnp.int32),
            pltpu.VMEM((rows, columns), jnp.int32),
            pltpu.VMEM((rows, columns), jnp.int32),
            pltpu.VMEM((3 * ocean_rows + 2 * rows, columns), F32),
            pltpu.VMEM((tiles, 3 * ocean_rows + 2 * rows, columns), F32),
            pltpu.VMEM((lines, rows, columns), F32),
            pltpu.VMEM((rows, lines, columns), F32),
            pltpu.VMEM((lines, rows, columns), F32),
            pltpu.VMEM((rows, lines, columns), F32),
            pltpu.VMEM((3, rows, 2 * columns), F32),
            pltpu.VMEM((4, extent, GROUP, columns), F32),
            pltpu.VMEM((5, lines, columns), F32),
            pltpu.VMEM((2, NFREQ, columns), F32),
            pltpu.VMEM((tiles, columns, rows * columns), BF16),
            pltpu.VMEM((3, rows, GROUP, columns), F32),
            pltpu.VMEM((sects, 3 * rows, columns), F32),
            pltpu.VMEM((tiles, 3 * rows, columns), F32),
            dma((8,)),
            dma,
            dma,
            dma((2, CHUNKS)),
            dma((2, CHUNKS)),
            dma((tiles,)),
            dma((tiles,)),
            dma((sects,)),
            dma((sects,)),
            dma((tiles,)),
            dma((tiles,)),
        ],
        compiler_params=pltpu.CompilerParams(
            collective_id=0, has_side_effects=True, vmem_limit_bytes=60 * 1024 * 1024
        ),
        cost_estimate=pl.CostEstimate(
            flops=bins * rows * columns * 200, bytes_accessed=8 * bins * rows * columns,
            transcendentals=0,
        ),
        name="coupling",
    )(
        jnp.asarray(np.concatenate([np.cos(angles), np.sin(angles), np.zeros(8)]), F32),
        courant,
        group_ratio,
        ocean_currents,
        elevation.reshape(ocean_rows, columns),
        sea_mask,
        owner_tile.reshape(rows, columns),
        ocean_slot.reshape(rows, columns),
        spectrum,
    )
    return pl.pallas_call(
        hand_on,
        out_shape=(
            jax.ShapeDtypeStruct(new_spectrum.shape, F32),
            jax.ShapeDtypeStruct(stress.shape, F32),
        ),
        in_specs=[hbm, hbm],
        out_specs=(hbm, hbm),
        scratch_shapes=[
            pltpu.VMEM(new_spectrum.shape, F32),
            pltpu.VMEM(stress.shape, F32),
            dma((COPIES + 1,)),
            dma((COPIES + 1,)),
        ],
        compiler_params=pltpu.CompilerParams(vmem_limit_bytes=60 * 1024 * 1024),
        name="hand_on",
    )(new_spectrum, stress)


def solution(mesh):
    in_specs = (
        P("sect", "tile", None),
        P(),
        P(),
        P(None, "tile"),
        P("tile"),
        P("tile", None),
        P("tile", None),
        P("tile"),
    )
    out_specs = (P("sect", "tile", None), P(None, "tile"))
    return jax.shard_map(local, mesh=mesh, in_specs=in_specs, out_specs=out_specs, check_vma=False)
```
